256 devices in a mesh: dp: 8 (over x, core), proto: 32 (over z, y).
Axes of the slice: x: 4, y: 4, z: 8, core: 2. Of those that a mesh axis runs over, the one named last changes fastest.
Arguments:
- teacher_emb: bfloat16 [4096, 256], P('dp'), may hold values from -6 to 6
- student_emb: bfloat16 [4096, 256], P('dp'), may hold values from -0.375 to 0.375
- prototypes: bfloat16 [256, 262144], P(None, ('dp', 'proto')), may hold values from -0.375 to 0.375
Outputs:
- total_loss: float32 [], replicated
- grad_student: float32 [4096, 256], P('dp')
- grad_prototypes: float32 [256, 262144], P(None, ('dp', 'proto'))
The draws below stay inside these ranges and needn't reach their ends.
All inputs are finite; a program needn't handle non-finite values.
Results may differ from the reference program's by a relative error of at most 0.0089.
Values may be sent and summed in bfloat16 or wider, within the bound.
A program may use at most 128 MiB of HBM per device.

```python
import math
import jax
import jax.numpy as jnp
from jax import lax

K = 256
PROTO_DEV = 1024
ITERS = 3
ROWS = 4096
PROTOS = 262144


def centre_table(key):
    return jax.random.truncated_normal(key, -4.0, 4.0, (64, K), jnp.float32)


def crop_centres(key):
    pick_key = jax.random.fold_in(key, 101)
    picks = jnp.min(jax.random.randint(pick_key, (3, ROWS), 0, 64), axis=0)
    return centre_table(key)[picks]


def draw_teacher_emb(key, part):
    chosen = crop_centres(key)
    key = jax.random.fold_in(key, 7)
    noise_key, mix_key = jax.random.split(key, 2)
    noise = jax.random.truncated_normal(noise_key, -4.0, 4.0, (ROWS, K), jnp.float32)
    strength = jax.random.uniform(mix_key, (ROWS, 1), jnp.float32, 0.5, 0.9)
    mixed = strength * chosen + jnp.sqrt(1.0 - strength * strength) * noise
    return mixed.astype(jnp.bfloat16)


def draw_student_emb(key, part):
    chosen = crop_centres(key)
    key = jax.random.fold_in(key, 11)
    noise_key, mix_key = jax.random.split(key, 2)
    noise = jax.random.truncated_normal(noise_key, -4.0, 4.0, (ROWS, K), jnp.float32)
    strength = jax.random.uniform(mix_key, (ROWS, 1), jnp.float32, 0.4, 0.8)
    mixed = strength * chosen + jnp.sqrt(1.0 - strength * strength) * noise
    return (0.0625 * mixed).astype(jnp.bfloat16)


def draw_prototypes(key, part):
    centres = centre_table(key)
    key = jax.random.fold_in(key, 13)
    pick_key, noise_key = jax.random.split(key, 2)
    block_picks = jax.random.randint(pick_key, (PROTOS // PROTO_DEV,), 0, 64)
    picks = jnp.repeat(block_picks, PROTO_DEV)
    chosen = centres[picks]
    noise = jax.random.truncated_normal(noise_key, -4.0, 4.0, (PROTOS, K), jnp.float32)
    mixed = 0.6 * chosen + 0.8 * noise
    return (0.0625 * mixed).T.astype(jnp.bfloat16)


def setup_inputs(seed: int = 0) -> dict:
    key_list = jax.random.split(jax.random.key(seed), 4)
    return {
        "teacher_emb": draw_teacher_emb(jax.random.fold_in(key_list[3], 71), 0),
        "student_emb": draw_student_emb(jax.random.fold_in(key_list[3], 71), 0),
        "prototypes": draw_prototypes(jax.random.fold_in(key_list[3], 71), 0),
    }


TEACHER_TEMP = 0.04
STUDENT_TEMP = 0.1
NORM_EPS = 1e-06

def unit_along(values, axis_index):
    floats = values.astype(jnp.float32)
    inverse = lax.rsqrt(lax.optimization_barrier(jnp.sum(floats * floats, axis=axis_index, keepdims=True)) + NORM_EPS)
    return (floats * inverse, inverse)

def reference(teacher_emb, student_emb, prototypes):
    teach_hat = unit_along(teacher_emb, 1)[0].astype(jnp.bfloat16)
    stud_unit, stud_inverse = unit_along(student_emb, 1)
    stud_hat = stud_unit.astype(jnp.bfloat16)
    proto_unit, proto_inverse = unit_along(prototypes, 0)
    proto_hat = proto_unit.astype(jnp.bfloat16)
    col_block = min(8192, PROTOS)
    block_count = PROTOS // col_block
    stacked = proto_hat.reshape(K, block_count, col_block).transpose(1, 0, 2)

    def teacher_exp(weights):
        return jnp.exp(jnp.dot(teach_hat, weights, preferred_element_type=jnp.float32) / TEACHER_TEMP)

    def student_logits(weights):
        return jnp.dot(stud_hat, weights, preferred_element_type=jnp.float32) / STUDENT_TEMP
    row_scale = jnp.ones((ROWS,), jnp.float32)
    col_scale = jnp.ones((PROTOS,), jnp.float32)
    for step_index in range(ITERS):
        current_rows = row_scale

        def column_mass(weights):
            return lax.optimization_barrier(jnp.sum(current_rows[:, None] * teacher_exp(weights), axis=0))
        col_scale = 1.0 / (PROTOS * lax.map(column_mass, stacked).reshape(PROTOS))

        def row_mass(pair):
            weights, scales = pair
            return lax.optimization_barrier(jnp.sum(teacher_exp(weights) * scales[None, :], axis=1))
        row_total = lax.optimization_barrier(jnp.sum(lax.map(row_mass, (stacked, col_scale.reshape(block_count, col_block))), axis=0))
        row_scale = 1.0 / (ROWS * row_total)

    def student_mass(weights):
        return lax.optimization_barrier(jnp.sum(jnp.exp(student_logits(weights)), axis=1))
    lse = jnp.log(lax.optimization_barrier(jnp.sum(lax.map(student_mass, stacked), axis=0)))

    def final_block(carry, pair):
        cross_acc, grad_acc = carry
        weights, scales = pair
        targets = ROWS * row_scale[:, None] * teacher_exp(weights) * scales[None, :]
        logits = student_logits(weights)
        probs = jnp.exp(logits - lse[:, None])
        delta = ((probs - targets) / STUDENT_TEMP).astype(jnp.bfloat16)
        cross_acc = cross_acc + lax.optimization_barrier(jnp.sum(targets * logits, axis=1))
        grad_acc = grad_acc + lax.dot_general(delta, weights, (((1,), (1,)), ((), ())), preferred_element_type=jnp.float32)
        weight_grad = lax.dot_general(stud_hat, delta, (((0,), (0,)), ((), ())), preferred_element_type=jnp.float32)
        return ((cross_acc, grad_acc), weight_grad)
    init = (jnp.zeros((ROWS,), jnp.float32), jnp.zeros((ROWS, K), jnp.float32))
    (cross_terms, dz_hat), weight_blocks = lax.scan(final_block, init, (stacked, col_scale.reshape(block_count, col_block)))
    dw_hat = weight_blocks.transpose(1, 0, 2).reshape(K, PROTOS)
    total_loss = jnp.mean(lse - cross_terms)
    grad_student = stud_inverse * (dz_hat - stud_unit * lax.optimization_barrier(jnp.sum(stud_unit * dz_hat, axis=1, keepdims=True)))
    grad_prototypes = PROTOS / math.sqrt(ROWS) * proto_inverse * (dw_hat - proto_unit * lax.optimization_barrier(jnp.sum(proto_unit * dw_hat, axis=0, keepdims=True)))
    return (total_loss, grad_student, grad_prototypes)
```

```python
import functools
import math

import jax
import jax.numpy as jnp
from jax import lax
from jax.experimental import pallas as pl
from jax.experimental.pallas import tpu as pltpu
from jax.sharding import PartitionSpec as P

ITERS = 3
TEACHER_TEMP = 0.04
STUDENT_TEMP = 0.1
NORM_EPS = 1e-06
LOG2E = 1.4426950408889634
NX, NC, NY, NZ = 4, 2, 4, 8

MESH = pl.DeviceIdType.MESH
F32, BF16 = jnp.float32, jnp.bfloat16
NT = (((1,), (1,)), ((), ()))


def unit_along(values, axis):
    floats = values.astype(F32)
    inverse = lax.rsqrt(jnp.sum(floats * floats, axis=axis, keepdims=True) + NORM_EPS)
    return floats * inverse, inverse


def split_rows(vec):
    n = vec.shape[1]
    high = vec.astype(BF16).astype(F32)
    low = vec - high
    row = lax.broadcasted_iota(jnp.int32, (16, n), 0)
    both = jnp.where(row == 0, high, jnp.where(row == 1, low, 0.0))
    return both.astype(BF16)


def kernel(
    total_rows,
    total_cols,
    teach_ref,
    stud_ref,
    proto_ref,
    loss_ref,
    gs_ref,
    gp_ref,
    teach_all,
    stud_all,
    proto_all,
    protot_all,
    exp_t,
    exp_s,
    acc,
    colx,
    xy1,
    z1,
    xy2,
    z2,
    send_a,
    send_b,
    recv_a,
    recv_b,
    send_a2,
    send_b2,
    recv_a2,
    recv_b2,
    zsend,
    zrecv,
    ygather,
    dw_buf,
    dw_send,
    dw_recv,
    loss_x,
    dzt,
    ssem,
    rsem,
):
    d = lax.axis_index("dp")
    p = lax.axis_index("proto")
    x, c = d // NC, lax.rem(d, NC)
    z, y = p // NY, lax.rem(p, NY)
    own = teach_ref.shape[0]
    k_dim, cols = proto_ref.shape
    rows = NX * own
    both_cols = 2 * cols

    def at_x(k):
        return lax.rem(x + k, NX)

    def at_y(k):
        return lax.rem(y + k, NY)

    def at_z(k):
        return lax.rem(z + k, NZ)

    def dev(xx, cc, yy, zz):
        return (xx * NC + cc, zz * NY + yy)

    partner = dev(x, 1 - c, y, z)
    xy_peers = [dev(at_x(k // 4), c, at_y(k % 4), z) for k in range(1, 16)]
    z_peers = [dev(x, c, y, at_z(k)) for k in range(1, 8)]

    barrier = pltpu.get_barrier_semaphore()
    everyone = [partner] + xy_peers + z_peers
    for peer in everyone:
        pl.semaphore_signal(barrier, inc=1, device_id=peer, device_id_type=MESH)

    started = []

    def send(src, dst, peer):
        index = len(started)
        copy = pltpu.make_async_remote_copy(
            src_ref=src,
            dst_ref=dst,
            send_sem=ssem.at[index],
            recv_sem=rsem.at[index],
            device_id=peer,
            device_id_type=MESH,
        )
        copy.start()
        started.append(copy)
        return index

    def arrive(index, landed, peer):
        pltpu.make_async_remote_copy(
            src_ref=landed,
            dst_ref=landed,
            send_sem=ssem.at[index],
            recv_sem=rsem.at[index],
            device_id=peer,
            device_id_type=MESH,
        ).wait_recv()

    X_ORDER = (1, 3, 2)

    teach_hat = unit_along(teach_ref[...], 1)[0]
    teach_all[x] = jnp.transpose(teach_hat).astype(BF16)
    pl.semaphore_wait(barrier, len(everyone))
    teach_copy = {
        k: send(teach_all.at[x], teach_all.at[x], dev(at_x(k), c, y, z)) for k in X_ORDER
    }
    proto_unit, proto_inverse = unit_along(proto_ref[...], 0)
    proto_all[c] = proto_unit.astype(BF16)
    protot_all[c] = jnp.transpose(proto_unit).astype(BF16)
    protot_copy = send(protot_all.at[c], protot_all.at[c], partner)
    proto_copy = send(proto_all.at[c], proto_all.at[c], partner)
    stud_hat = unit_along(stud_ref[...], 1)[0]
    stud_all[x] = jnp.transpose(stud_hat).astype(BF16)
    stud_copy = {
        k: send(stud_all.at[x], stud_all.at[x], dev(at_x(k), c, y, z)) for k in X_ORDER
    }

    CH = 512
    half_steps = cols // CH

    def teacher_block(block, half):
        def body(i, carry):
            rows_in = pl.ds(pl.multiple_of(i * CH, CH), CH)
            rows_out = pl.ds(pl.multiple_of(half * cols + i * CH, CH), CH)
            prod = jnp.dot(
                protot_all[half, rows_in, :], teach_all[block], preferred_element_type=F32
            )
            e = jnp.exp2(prod * (LOG2E / TEACHER_TEMP))
            exp_t[block, rows_out, :] = e.astype(BF16)
            part = e[:, 0:128]
            for lane in range(128, own, 128):
                part = part + e[:, lane : lane + 128]
            acc[rows_out, :] += part
            return carry

        lax.fori_loop(0, half_steps, body, 0)

    acc[...] = jnp.zeros_like(acc)
    teacher_block(x, c)
    arrive(protot_copy, protot_all.at[1 - c], partner)
    teacher_block(x, 1 - c)
    for k in X_ORDER:
        source = at_x(NX - k)
        arrive(teach_copy[k], teach_all.at[source], dev(source, c, y, z))
        teacher_block(source, 0)
        teacher_block(source, 1)

    def column_scale(step, sums):
        colx[step, c] = sums
        index = send(colx.at[step, c], colx.at[step, c], partner)
        arrive(index, colx.at[step, 1 - c], partner)
        return 1.0 / (total_cols * (colx[step, 0] + colx[step, 1]))

    def first_column_sums():
        parts = []
        for b in range(both_cols // 128):
            t = jnp.transpose(acc[b * 128 : (b + 1) * 128, :])
            parts.append(jnp.sum(t, axis=0, keepdims=True))
        return jnp.concatenate(parts, axis=1)

    def column_sums(row_scale):
        left = split_rows(row_scale)
        total = None
        for j in range(NX):
            part = lax.dot_general(
                left[:, j * own : (j + 1) * own], exp_t[j], NT, preferred_element_type=F32
            )
            total = part if total is None else total + part
        return total[0:1] + total[1:2]

    def row_sums(col_scale):
        left = split_rows(col_scale)
        parts = []
        for j in range(NX):
            part = jnp.dot(left, exp_t[j], preferred_element_type=F32)
            parts.append(part[0:1] + part[1:2])
        return jnp.concatenate(parts, axis=1)

    xy_me = x * NY + y

    def start_xy(buf, vec):
        buf[xy_me] = vec
        return [send(buf.at[xy_me], buf.at[xy_me], peer) for peer in xy_peers]

    def finish_xy(buf, indices):
        for k, index in zip(range(1, 16), indices):
            sx, sy = at_x(NX - k // 4), at_y(NY - k % 4)
            arrive(index, buf.at[sx * NY + sy], dev(sx, c, sy, z))
        total = buf[0]
        for i in range(1, 16):
            total = total + buf[i]
        return total

    def start_z(buf, vec):
        buf[z] = vec
        return [send(buf.at[z], buf.at[z], peer) for peer in z_peers]

    def finish_z(buf, indices):
        for k, index in zip(range(1, 8), indices):
            sz = at_z(NZ - k)
            arrive(index, buf.at[sz], dev(x, c, y, sz))
        total = buf[0]
        for i in range(1, 8):
            total = total + buf[i]
        return total

    half_k, piece = k_dim // 2, k_dim // 8

    def reduce_block(which, j, value):
        low = value.astype(BF16)
        send_a[which, j] = low[:half_k]
        for q in range(NY):
            send_b[which, q, j] = low[half_k + q * piece : half_k + (q + 1) * piece]

    def start_first(which):
        a = {
            k: send(send_a.at[which, at_x(k)], recv_a.at[which, x], dev(at_x(k), c, y, z))
            for k in X_ORDER
        }
        b = {
            k: send(send_b.at[which, at_y(k)], recv_b.at[which, y], dev(x, c, at_y(k), z))
            for k in X_ORDER
        }
        return a, b

    def start_second(which, first):
        a, b = first
        recv_a[which, x] = send_a[which, x]
        recv_b[which, y] = send_b[which, y]
        for k in X_ORDER:
            source = at_x(NX - k)
            arrive(a[k], recv_a.at[which, source], dev(source, c, y, z))
        total = recv_a[which, 0].astype(F32)
        for i in range(1, NX):
            total = total + recv_a[which, i].astype(F32)
        low = total.astype(BF16)
        for q in range(NY):
            send_a2[which, q] = low[q * piece : (q + 1) * piece]
        a2 = {
            k: send(send_a2.at[which, at_y(k)], recv_a2.at[which, y], dev(x, c, at_y(k), z))
            for k in X_ORDER
        }
        for k in X_ORDER:
            source = at_y(NY - k)
            arrive(b[k], recv_b.at[which, source], dev(x, c, source, z))
        for j in range(NX):
            total = recv_b[which, 0, j].astype(F32)
            for i in range(1, NY):
                total = total + recv_b[which, i, j].astype(F32)
            send_b2[which, j] = total.astype(BF16)
        b2 = {
            k: send(send_b2.at[which, at_x(k)], recv_b2.at[which, x], dev(at_x(k), c, y, z))
            for k in X_ORDER
        }
        return a2, b2

    def finish_second(which, second):
        a2, b2 = second
        recv_a2[which, y] = send_a2[which, y]
        recv_b2[which, x] = send_b2[which, x]
        for k in X_ORDER:
            source = at_y(NY - k)
            arrive(a2[k], recv_a2.at[which, source], dev(x, c, source, z))
        for k in X_ORDER:
            source = at_x(NX - k)
            arrive(b2[k], recv_b2.at[which, source], dev(source, c, y, z))
        low = recv_a2[which, 0].astype(F32)
        high = recv_b2[which, 0].astype(F32)
        for i in range(1, 4):
            low = low + recv_a2[which, i].astype(F32)
            high = high + recv_b2[which, i].astype(F32)
        return jnp.concatenate([low, high], axis=0)

    scale = column_scale(0, first_column_sums())
    xy_copies = start_xy(xy1, row_sums(scale))

    arrive(proto_copy, proto_all.at[1 - c], partner)
    for k in X_ORDER:
        source = at_x(NX - k)
        arrive(stud_copy[k], stud_all.at[source], dev(source, c, y, z))

    def student_body(i, carry):
        block, chunk = i // (2 * half_steps), lax.rem(i, 2 * half_steps)
        half, inner = chunk // half_steps, lax.rem(chunk, half_steps)
        prod = jnp.dot(
            protot_all[half, pl.ds(pl.multiple_of(inner * CH, CH), CH), :],
            stud_all[block],
            preferred_element_type=F32,
        )
        exp_s[block, pl.ds(pl.multiple_of(chunk * CH, CH), CH), :] = jnp.exp2(
            prod * (LOG2E / STUDENT_TEMP)
        ).astype(BF16)
        return carry

    lax.fori_loop(0, NX * 2 * half_steps, student_body, 0)

    z_copies = start_z(z1, finish_xy(xy1, xy_copies))

    protos = jnp.concatenate([proto_all[0], proto_all[1]], axis=1)
    ones = jnp.ones((16, both_cols), BF16)
    stud_sums = []
    for j in range(NX):
        reduce_block(0, j, jnp.dot(protos, exp_s[j], preferred_element_type=F32))
        stud_sums.append(jnp.dot(ones, exp_s[j], preferred_element_type=F32)[0:1])
    first_p1 = start_first(0)
    row_scale = 1.0 / (total_rows * finish_z(z1, z_copies))

    scale = column_scale(1, column_sums(row_scale))
    vec = jnp.concatenate([row_sums(scale), jnp.concatenate(stud_sums, axis=1)], axis=0)
    xy_copies = start_xy(xy2.at[0], vec)
    second_p1 = start_second(0, first_p1)
    z_copies = start_z(z2.at[0], finish_xy(xy2.at[0], xy_copies))
    totals = finish_z(z2.at[0], z_copies)
    row_scale = 1.0 / (total_rows * totals[0:1])
    stud_total = totals[1:2]

    scale = column_scale(2, column_sums(row_scale))
    sums = row_sums(scale)
    scaled = (protos.astype(F32) * scale).astype(BF16)
    cross = []
    for j in range(NX):
        value = jnp.dot(scaled, exp_t[j], preferred_element_type=F32)
        reduce_block(1, j, value)
        cross.append(jnp.sum(value * stud_all[j].astype(F32), axis=0, keepdims=True))
    first_p2 = start_first(1)
    vec = jnp.concatenate([sums, jnp.concatenate(cross, axis=1)], axis=0)
    xy_copies = start_xy(xy2.at[1], vec)

    stud_factor = (1.0 / STUDENT_TEMP) / stud_total
    for h in range(2):
        total = None
        for j in range(NX):
            left = (stud_all[j].astype(F32) * stud_factor[:, j * own : (j + 1) * own]).astype(BF16)
            part = lax.dot_general(
                left, exp_s[j, h * cols : (h + 1) * cols, :], NT, preferred_element_type=F32
            )
            total = part if total is None else total + part
        dw_buf[h] = total

    z_copies = start_z(z2.at[1], finish_xy(xy2.at[1], xy_copies))
    second_p2 = start_second(1, first_p2)
    totals = finish_z(z2.at[1], z_copies)
    row_scale = 1.0 / (total_rows * totals[0:1])
    teach_factor = (total_rows / STUDENT_TEMP) * row_scale

    terms = jnp.log(stud_total) - teach_factor * totals[1:2]
    part = terms[:, 0:128]
    for lane in range(128, rows, 128):
        part = part + terms[:, lane : lane + 128]
    loss_x[c] = part
    loss_copy = send(loss_x.at[c], loss_x.at[c], partner)

    loss_x_dummy = None
    acc_rows = stud_factor[:, 0:own]
    acc_rows2 = teach_factor[:, 0:own]
    for j in range(1, NX):
        acc_rows = jnp.where(x == j, stud_factor[:, j * own : (j + 1) * own], acc_rows)
        acc_rows2 = jnp.where(x == j, teach_factor[:, j * own : (j + 1) * own], acc_rows2)
    mixed = acc_rows * finish_second(0, second_p1) - acc_rows2 * finish_second(1, second_p2)
    low = mixed.astype(BF16)
    half_own = own // 2
    for q in range(NZ):
        r = 16 * (q // 2)
        s = half_own * (q % 2)
        zsend[q] = low[r : r + 16, s : s + half_own]
    z_copies = [
        send(zsend.at[at_z(k)], zrecv.at[z], dev(x, c, y, at_z(k))) for k in range(1, NZ)
    ]

    for h in range(2):
        total = None
        for j in range(NX):
            left = (stud_all[j].astype(F32) * teach_factor[:, j * own : (j + 1) * own]).astype(BF16)
            part = lax.dot_general(
                left, exp_t[j, h * cols : (h + 1) * cols, :], NT, preferred_element_type=F32
            )
            total = part if total is None else total + part
        dw_buf[h] = dw_buf[h] - total * scale[:, h * cols : (h + 1) * cols]
    dw_send[...] = dw_buf[1 - c].astype(BF16)
    dw_copy = send(dw_send, dw_recv, partner)

    zrecv[z] = zsend[z]
    for k in range(1, NZ):
        sz = at_z(NZ - k)
        arrive(z_copies[k - 1], zrecv.at[sz], dev(x, c, y, sz))
    total = zrecv[0].astype(F32)
    for i in range(1, NZ):
        total = total + zrecv[i].astype(F32)
    ygather[y, z] = total.astype(BF16)
    z_copies = [
        send(ygather.at[y, z], ygather.at[y, z], dev(x, c, y, at_z(k))) for k in range(1, NZ)
    ]

    arrive(loss_copy, loss_x.at[1 - c], partner)
    loss_ref[...] = jnp.broadcast_to(
        jnp.sum(loss_x[0] + loss_x[1], axis=1, keepdims=True) / total_rows, loss_ref.shape
    )
    arrive(dw_copy, dw_recv, partner)
    dw_hat = dw_buf[c] + dw_recv[...].astype(F32)
    proto_unit, proto_inverse = unit_along(proto_ref[...], 0)
    gp_ref[...] = (
        (total_cols / math.sqrt(total_rows))
        * proto_inverse
        * (dw_hat - proto_unit * jnp.sum(proto_unit * dw_hat, axis=0, keepdims=True))
    )

    for k in range(1, NZ):
        sz = at_z(NZ - k)
        arrive(z_copies[k - 1], ygather.at[y, sz], dev(x, c, y, sz))
    y_copies = {
        k: send(ygather.at[y], ygather.at[y], dev(x, c, at_y(k), z)) for k in X_ORDER
    }
    for k in X_ORDER:
        source = at_y(NY - k)
        arrive(y_copies[k], ygather.at[source], dev(x, c, source, z))
    for i in range(NY):
        for q in range(NZ):
            r = 16 * (q // 2)
            s = half_own * (q % 2)
            base = i * piece + r if r < piece else half_k + i * piece + r - piece
            dzt[base : base + 16, s : s + half_own] = ygather[i, q].astype(F32)
    dz = jnp.transpose(dzt[...])
    stud_unit, stud_inverse = unit_along(stud_ref[...], 1)
    gs_ref[...] = stud_inverse * (
        dz - stud_unit * jnp.sum(stud_unit * dz, axis=1, keepdims=True)
    )
    for copy in started:
        copy.wait_send()


def solution(mesh):
    def shards(teacher_emb, student_emb, prototypes):
        own, k_dim = teacher_emb.shape
        cols = prototypes.shape[1]
        rows, both = NX * own, 2 * cols
        total_rows = own * mesh.shape["dp"]
        total_cols = cols * mesh.shape["dp"] * mesh.shape["proto"]
        vmem = pltpu.VMEM
        piece = k_dim // 8
        scratch = [
            vmem((NX, k_dim, own), BF16),
            vmem((NX, k_dim, own), BF16),
            vmem((NC, k_dim, cols), BF16),
            vmem((NC, cols, k_dim), BF16),
            vmem((NX, both, own), BF16),
            vmem((NX, both, own), BF16),
            vmem((both, 128), F32),
            vmem((ITERS, NC, 1, both), F32),
            vmem((NX * NY, 1, rows), F32),
            vmem((NZ, 1, rows), F32),
            vmem((2, NX * NY, 2, rows), F32),
            vmem((2, NZ, 2, rows), F32),
            vmem((2, NX, k_dim // 2, own), BF16),
            vmem((2, NY, NX, piece, own), BF16),
            vmem((2, NX, k_dim // 2, own), BF16),
            vmem((2, NY, NX, piece, own), BF16),
            vmem((2, NY, piece, own), BF16),
            vmem((2, NX, piece, own), BF16),
            vmem((2, NY, piece, own), BF16),
            vmem((2, NX, piece, own), BF16),
            vmem((NZ, 16, own // 2), BF16),
            vmem((NZ, 16, own // 2), BF16),
            vmem((NY, NZ, 16, own // 2), BF16),
            vmem((2, k_dim, cols), F32),
            vmem((k_dim, cols), BF16),
            vmem((k_dim, cols), BF16),
            vmem((2, 1, 128), F32),
            vmem((k_dim, own), F32),
            pltpu.SemaphoreType.DMA((160,)),
            pltpu.SemaphoreType.DMA((160,)),
        ]
        loss, grad_student, grad_prototypes = pl.pallas_call(
            functools.partial(kernel, float(total_rows), float(total_cols)),
            out_shape=(
                jax.ShapeDtypeStruct((1, 128), F32),
                jax.ShapeDtypeStruct((own, k_dim), F32),
                jax.ShapeDtypeStruct((k_dim, cols), F32),
            ),
            in_specs=[pl.BlockSpec(memory_space=vmem)] * 3,
            out_specs=[pl.BlockSpec(memory_space=vmem)] * 3,
            scratch_shapes=scratch,
            compiler_params=pltpu.CompilerParams(
                collective_id=0, has_side_effects=True, vmem_limit_bytes=60 << 20
            ),
            name="prototype_head",
        )(teacher_emb, student_emb, prototypes)
        return loss[0, 0], grad_student, grad_prototypes

    in_specs = (P("dp", None), P("dp", None), P(None, ("dp", "proto")))
    out_specs = (P(), P("dp", None), P(None, ("dp", "proto")))
    return jax.shard_map(shards, mesh=mesh, in_specs=in_specs, out_specs=out_specs, check_vma=False)
```

```python
import functools
import math

import jax
import jax.numpy as jnp
from jax import lax
from jax.experimental import pallas as pl
from jax.experimental.pallas import tpu as pltpu
from jax.sharding import PartitionSpec as P

ITERS = 3
TEACHER_TEMP = 0.04
STUDENT_TEMP = 0.1
NORM_EPS = 1e-06
LOG2E = 1.4426950408889634
NX, NC, NY, NZ = 4, 2, 4, 8

MESH = pl.DeviceIdType.MESH
scope = jax.named_scope
F32, BF16 = jnp.float32, jnp.bfloat16
NT = (((1,), (1,)), ((), ()))


def unit_along(values, axis):
    floats = values.astype(F32)
    inverse = lax.rsqrt(jnp.sum(floats * floats, axis=axis, keepdims=True) + NORM_EPS)
    return floats * inverse, inverse


def split_rows(vec):
    n = vec.shape[1]
    high = vec.astype(BF16).astype(F32)
    low = vec - high
    row = lax.broadcasted_iota(jnp.int32, (16, n), 0)
    both = jnp.where(row == 0, high, jnp.where(row == 1, low, 0.0))
    return both.astype(BF16)


def kernel(
    total_rows,
    total_cols,
    teach_ref,
    stud_ref,
    proto_ref,
    loss_ref,
    gs_ref,
    gp_ref,
    teach_all,
    stud_all,
    proto_all,
    protot_all,
    left,
    exp_t,
    exp_s,
    acc,
    colx,
    xy_vec,
    z_vec,
    xy_loss,
    z_loss,
    send_a,
    send_b,
    recv_a,
    recv_b,
    send_a2,
    send_b2,
    recv_a2,
    recv_b2,
    zsend,
    zrecv,
    ygather,
    cross,
    fac_mix,
    dw_buf,
    dw_send,
    dw_recv,
    loss_x,
    dzt,
    ssem,
    rsem,
):
    d = lax.axis_index("dp")
    p = lax.axis_index("proto")
    x, c = d // NC, lax.rem(d, NC)
    z, y = p // NY, lax.rem(p, NY)
    own = teach_ref.shape[0]
    k_dim, cols = proto_ref.shape
    rows = NX * own
    both_cols = 2 * cols
    half_own = own // 2

    def at_x(k):
        return lax.rem(x + k, NX)

    def at_y(k):
        return lax.rem(y + k, NY)

    def at_z(k):
        return lax.rem(z + k, NZ)

    def dev(xx, cc, yy, zz):
        return (xx * NC + cc, zz * NY + yy)

    def x_dev(xx):
        return dev(xx, c, y, z)

    def y_dev(yy):
        return dev(x, c, yy, z)

    def z_dev(zz):
        return dev(x, c, y, zz)

    partner = dev(x, 1 - c, y, z)
    xy_peers = [dev(at_x(k // 4), c, at_y(k % 4), z) for k in range(1, 16)]
    z_peers = [z_dev(at_z(k)) for k in range(1, 8)]
    everyone = [partner] + xy_peers + z_peers
    AROUND = (2, 1, 3)

    barrier = pltpu.get_barrier_semaphore()
    for peer in everyone:
        pl.semaphore_signal(barrier, inc=1, device_id=peer, device_id_type=MESH)

    started = []

    def send(src, dst, peer):
        index = len(started)
        copy = pltpu.make_async_remote_copy(
            src_ref=src,
            dst_ref=dst,
            send_sem=ssem.at[index],
            recv_sem=rsem.at[index],
            device_id=peer,
            device_id_type=MESH,
        )
        copy.start()
        started.append(copy)
        return index

    def arrive(index, landed, peer):
        pltpu.make_async_remote_copy(
            src_ref=landed,
            dst_ref=landed,
            send_sem=ssem.at[index],
            recv_sem=rsem.at[index],
            device_id=peer,
            device_id_type=MESH,
        ).wait_recv()

    def start_gather(blocks):
        far = send(blocks.at[x, y], blocks.at[x, y], x_dev(at_x(2)))
        return far, {k: send(blocks.at[x], blocks.at[x], x_dev(at_x(k))) for k in (1, 3)}

    def relay_far(blocks, copies):
        source = at_x(2)
        arrive(copies[0], blocks.at[source, y], x_dev(source))
        return {
            k: send(blocks.at[source, y], blocks.at[source, y], y_dev(at_y(k))) for k in AROUND
        }

    def finish_far(blocks, relays):
        source = at_x(2)
        for k in AROUND:
            sy = at_y(NY - k)
            arrive(relays[k], blocks.at[source, sy], y_dev(sy))

    def block_of(blocks, j):
        return blocks[j].reshape(k_dim, own)

    with scope("s_norm"):
        teach_hat = unit_along(teach_ref[...], 1)[0]
        teach_all[x] = jnp.transpose(teach_hat).astype(BF16).reshape(4, k_dim // 4, own)
    with scope("s_barrier"):
        pl.semaphore_wait(barrier, len(everyone))
    with scope("s_norm"):
        teach_copies = start_gather(teach_all)
        proto_unit = unit_along(proto_ref[...], 0)[0]
        protot_all[c] = jnp.transpose(proto_unit).astype(BF16)
        protot_copy = send(protot_all.at[c], protot_all.at[c], partner)
        proto_all[c] = proto_unit.astype(BF16)
        proto_copy = send(proto_all.at[c], proto_all.at[c], partner)
        stud_hat = unit_along(stud_ref[...], 1)[0]
        stud_all[x] = jnp.transpose(stud_hat).astype(BF16).reshape(4, k_dim // 4, own)
        stud_copies = start_gather(stud_all)

    CH = 512
    half_steps = cols // CH

    def teacher_block(block, half):
        def body(i, carry):
            rows_in = pl.ds(pl.multiple_of(i * CH, CH), CH)
            rows_out = pl.ds(pl.multiple_of(half * cols + i * CH, CH), CH)
            prod = jnp.dot(
                protot_all[half, rows_in, :],
                block_of(teach_all, block),
                preferred_element_type=F32,
            )
            e = jnp.exp2(prod * (LOG2E / TEACHER_TEMP))
            exp_t[block, rows_out, :] = e.astype(BF16)
            part = e[:, 0:128]
            for lane in range(128, own, 128):
                part = part + e[:, lane : lane + 128]
            acc[rows_out, :] += part
            return carry

        lax.fori_loop(0, half_steps, body, 0)

    def student_block(block):
        def body(i, carry):
            half, inner = i // half_steps, lax.rem(i, half_steps)
            prod = jnp.dot(
                protot_all[half, pl.ds(pl.multiple_of(inner * CH, CH), CH), :],
                block_of(stud_all, block),
                preferred_element_type=F32,
            )
            exp_s[block, pl.ds(pl.multiple_of(i * CH, CH), CH), :] = jnp.exp2(
                prod * (LOG2E / STUDENT_TEMP)
            ).astype(BF16)
            return carry

        lax.fori_loop(0, 2 * half_steps, body, 0)

    with scope("s_T_own"):
        acc[...] = jnp.zeros_like(acc)
        teacher_block(x, c)
        arrive(protot_copy, protot_all.at[1 - c], partner)
        teacher_block(x, 1 - c)
    with scope("s_relay"):
        teach_relays = relay_far(teach_all, teach_copies)
    with scope("s_T_near"):
        for k in (1, 3):
            source = at_x(NX - k)
            arrive(teach_copies[1][k], teach_all.at[source], x_dev(source))
            teacher_block(source, 0)
            teacher_block(source, 1)
    with scope("s_relay"):
        stud_relays = relay_far(stud_all, stud_copies)
    with scope("s_T_far_wait"):
        finish_far(teach_all, teach_relays)
    with scope("s_T_far"):
        teacher_block(at_x(2), 0)
        teacher_block(at_x(2), 1)

    def column_scale(step, sums):
        colx[step, c] = sums
        index = send(colx.at[step, c], colx.at[step, c], partner)
        arrive(index, colx.at[step, 1 - c], partner)
        return 1.0 / (total_cols * (colx[step, 0] + colx[step, 1]))

    def first_column_sums():
        parts = []
        for b in range(both_cols // 128):
            t = jnp.transpose(acc[b * 128 : (b + 1) * 128, :])
            parts.append(jnp.sum(t, axis=0, keepdims=True))
        return jnp.concatenate(parts, axis=1)

    def column_sums(row_scale):
        both = split_rows(row_scale)
        total = None
        for j in range(NX):
            part = lax.dot_general(
                both[:, j * own : (j + 1) * own], exp_t[j], NT, preferred_element_type=F32
            )
            total = part if total is None else total + part
        return total[0:1] + total[1:2]

    def row_sums(col_scale):
        both = split_rows(col_scale)
        parts = []
        for j in range(NX):
            part = jnp.dot(both, exp_t[j], preferred_element_type=F32)
            parts.append(part[0:1] + part[1:2])
        return jnp.concatenate(parts, axis=1)

    xy_me = x * NY + y

    def start_xy(buf, vec):
        buf[xy_me] = vec
        return [send(buf.at[xy_me], buf.at[xy_me], peer) for peer in xy_peers]

    def finish_xy(buf, indices):
        for k, index in zip(range(1, 16), indices):
            sx, sy = at_x(NX - k // 4), at_y(NY - k % 4)
            arrive(index, buf.at[sx * NY + sy], dev(sx, c, sy, z))
        total = buf[0]
        for i in range(1, 16):
            total = total + buf[i]
        return total

    def start_z(buf, vec):
        buf[z] = vec
        return [send(buf.at[z], buf.at[z], peer) for peer in z_peers]

    def finish_z(buf, indices):
        for k, index in zip(range(1, 8), indices):
            sz = at_z(NZ - k)
            arrive(index, buf.at[sz], z_dev(sz))
        total = buf[0]
        for i in range(1, 8):
            total = total + buf[i]
        return total

    half_k, piece = k_dim // 2, k_dim // 8

    def put_block(which, j, value):
        low = value.astype(BF16)
        send_a[which, j] = low[:half_k]
        for q in range(NY):
            send_b[which, q, j] = low[half_k + q * piece : half_k + (q + 1) * piece]

    def send_block_a(which, k):
        j = at_x(k)
        return send(send_a.at[which, j], recv_a.at[which, x], x_dev(j))

    def send_block_b(which, k):
        j = at_x(k)
        return {
            h: send(send_b.at[which, at_y(h), j], recv_b.at[which, y, j], y_dev(at_y(h)))
            for h in AROUND
        }

    def start_second(which, a, b):
        recv_a[which, x] = send_a[which, x]
        recv_b[which, y] = send_b[which, y]
        for k in AROUND:
            source = at_x(NX - k)
            arrive(a[k], recv_a.at[which, source], x_dev(source))
        total = recv_a[which, 0].astype(F32)
        for i in range(1, NX):
            total = total + recv_a[which, i].astype(F32)
        low = total.astype(BF16)
        for q in range(NY):
            send_a2[which, q] = low[q * piece : (q + 1) * piece]
        a2 = {
            k: send(send_a2.at[which, at_y(k)], recv_a2.at[which, y], y_dev(at_y(k)))
            for k in AROUND
        }
        for k in b:
            for h in AROUND:
                source = at_y(NY - h)
                arrive(b[k][h], recv_b.at[which, source, at_x(k)], y_dev(source))
        for j in range(NX):
            total = recv_b[which, 0, j].astype(F32)
            for i in range(1, NY):
                total = total + recv_b[which, i, j].astype(F32)
            send_b2[which, j] = total.astype(BF16)
        b2 = {
            k: send(send_b2.at[which, at_x(k)], recv_b2.at[which, x], x_dev(at_x(k)))
            for k in AROUND
        }
        return a2, b2

    def start_third(which, second):
        a2, b2 = second
        recv_a2[which, y] = send_a2[which, y]
        recv_b2[which, x] = send_b2[which, x]
        for k in AROUND:
            source = at_y(NY - k)
            arrive(a2[k], recv_a2.at[which, source], y_dev(source))
        for k in AROUND:
            source = at_x(NX - k)
            arrive(b2[k], recv_b2.at[which, source], x_dev(source))
        low = recv_a2[which, 0].astype(F32)
        high = recv_b2[which, 0].astype(F32)
        for i in range(1, 4):
            low = low + recv_a2[which, i].astype(F32)
            high = high + recv_b2[which, i].astype(F32)
        low, high = low.astype(BF16), high.astype(BF16)
        for q in range(NZ):
            r = 16 * (q // 2)
            s = half_own * (q % 2)
            part = low[r : r + 16] if r < piece else high[r - piece : r - piece + 16]
            zsend[which, q] = part[:, s : s + half_own]
        return [
            send(zsend.at[which, at_z(k)], zrecv.at[which, z], z_dev(at_z(k)))
            for k in range(1, NZ)
        ]

    def finish_third(which, third):
        zrecv[which, z] = zsend[which, z]
        for k in range(1, NZ):
            sz = at_z(NZ - k)
            arrive(third[k - 1], zrecv.at[which, sz], z_dev(sz))
        total = zrecv[which, 0].astype(F32)
        for i in range(1, NZ):
            total = total + zrecv[which, i].astype(F32)
        return total

    with scope("s_col1"):
        scale = column_scale(0, first_column_sums())
    with scope("s_row1"):
        xy_copies = start_xy(xy_vec.at[0], row_sums(scale))
    with scope("s_S_near"):
        student_block(x)
        for k in (1, 3):
            source = at_x(NX - k)
            arrive(stud_copies[1][k], stud_all.at[source], x_dev(source))
            student_block(source)
    with scope("s_xy1"):
        z_copies = start_z(z_vec.at[0], finish_xy(xy_vec.at[0], xy_copies))
    with scope("s_S_far"):
        finish_far(stud_all, stud_relays)
        student_block(at_x(2))
    with scope("s_P1"):
        arrive(proto_copy, proto_all.at[1 - c], partner)
        left[0:k_dim, 0:cols] = proto_all[0]
        left[0:k_dim, cols:] = proto_all[1]
        left[k_dim:, :] = jnp.ones((16, both_cols), BF16)
        stud_sums = []
        for j in range(NX):
            value = jnp.dot(left[...], exp_s[j], preferred_element_type=F32)
            put_block(0, j, value[0:k_dim])
            stud_sums.append(value[k_dim : k_dim + 1])
        stud_xy = start_xy(xy_vec.at[3], jnp.concatenate(stud_sums, axis=1))
    with scope("s_z1"):
        row_scale = 1.0 / (total_rows * finish_z(z_vec.at[0], z_copies))

    with scope("s_col2"):
        sums = column_sums(row_scale)
    with scope("s_colx2"):
        scale = column_scale(1, sums)
    with scope("s_row2"):
        xy_copies = start_xy(xy_vec.at[1], row_sums(scale))
        a1 = {k: send_block_a(0, k) for k in AROUND}
        b1 = {k: send_block_b(0, k) for k in (0, 1, 2, 3)}
    with scope("s_studxy"):
        stud_z = start_z(z_vec.at[3], finish_xy(xy_vec.at[3], stud_xy))
    with scope("s_xy2"):
        z_copies = start_z(z_vec.at[1], finish_xy(xy_vec.at[1], xy_copies))
    with scope("s_second1"):
        second1 = start_second(0, a1, b1)
    with scope("s_z2"):
        row_scale = 1.0 / (total_rows * finish_z(z_vec.at[1], z_copies))

    with scope("s_col3"):
        sums = column_sums(row_scale)
    with scope("s_colx3"):
        scale = column_scale(2, sums)
    with scope("s_P2"):
        for h in range(NC):
            left[0:k_dim, h * cols : (h + 1) * cols] = (
                proto_all[h].astype(F32) * scale[:, h * cols : (h + 1) * cols]
            ).astype(BF16)
        left[k_dim:, :] = split_rows(scale)
        a2, b2 = {}, {}
        for k in (2, 1, 3, 0):
            j = at_x(k)
            value = jnp.dot(left[...], exp_t[j], preferred_element_type=F32)
            put_block(1, j, value[0:k_dim])
            if k:
                a2[k] = send_block_a(1, k)
            b2[k] = send_block_b(1, k)
            xy_vec[2, xy_me, :, pl.ds(pl.multiple_of(j * own, own), own)] = (
                value[k_dim : k_dim + 1] + value[k_dim + 1 : k_dim + 2]
            )
            cross[j] = jnp.sum(
                value[0:k_dim] * block_of(stud_all, j).astype(F32), axis=0, keepdims=True
            )
        xy_copies = [
            send(xy_vec.at[2, xy_me], xy_vec.at[2, xy_me], peer) for peer in xy_peers
        ]
    with scope("s_third1"):
        third1 = start_third(0, second1)

    with scope("s_dwS"):
        stud_total = finish_z(z_vec.at[3], stud_z)
        stud_factor = (1.0 / STUDENT_TEMP) / stud_total
        for h in range(NC):
            total = None
            for j in range(NX):
                weights = (
                    block_of(stud_all, j).astype(F32) * stud_factor[:, j * own : (j + 1) * own]
                ).astype(BF16)
                part = lax.dot_general(
                    weights,
                    exp_s[j, h * cols : (h + 1) * cols, :],
                    NT,
                    preferred_element_type=F32,
                )
                total = part if total is None else total + part
            dw_buf[h] = total
    with scope("s_xy3"):
        z_copies = start_z(z_vec.at[2], finish_xy(xy_vec.at[2], xy_copies))
    with scope("s_second2"):
        second2 = start_second(1, a2, b2)
    with scope("s_third2"):
        third2 = start_third(1, second2)
    with scope("s_z3"):
        row_scale = 1.0 / (total_rows * finish_z(z_vec.at[2], z_copies))
        teach_factor = (total_rows / STUDENT_TEMP) * row_scale

    with scope("s_loss"):
        part = None
        for j in range(NX):
            term = teach_factor[:, j * own : (j + 1) * own] * cross[j]
            for lane in range(0, own, 128):
                t = term[:, lane : lane + 128]
                part = t if part is None else part + t
        loss_xy = start_xy(xy_loss, part)

    with scope("s_mix"):
        part1 = finish_third(0, third1)
        part2 = finish_third(1, third2)
        for i in range(2 * NX):
            s = i * half_own
            fac_mix[0, i] = stud_factor[:, s : s + half_own]
            fac_mix[1, i] = teach_factor[:, s : s + half_own]
        mine = x * 2 + lax.rem(z, 2)
        ygather[y, z] = (fac_mix[0, mine] * part1 - fac_mix[1, mine] * part2).astype(BF16)
        gather_z = [
            send(ygather.at[y, z], ygather.at[y, z], z_dev(at_z(k))) for k in range(1, NZ)
        ]

    with scope("s_dwT"):
        for h in range(NC):
            total = None
            for j in range(NX):
                weights = (
                    block_of(stud_all, j).astype(F32) * teach_factor[:, j * own : (j + 1) * own]
                ).astype(BF16)
                part = lax.dot_general(
                    weights,
                    exp_t[j, h * cols : (h + 1) * cols, :],
                    NT,
                    preferred_element_type=F32,
                )
                total = part if total is None else total + part
            dw_buf[h] = dw_buf[h] - total * scale[:, h * cols : (h + 1) * cols]
        dw_send[...] = dw_buf[1 - c].astype(BF16)
        dw_copy = send(dw_send, dw_recv, partner)
    with scope("s_lossxy"):
        loss_z = start_z(z_loss, finish_xy(xy_loss, loss_xy))
    with scope("s_gatherz"):
        for k in range(1, NZ):
            sz = at_z(NZ - k)
            arrive(gather_z[k - 1], ygather.at[y, sz], z_dev(sz))
        gather_y = {k: send(ygather.at[y], ygather.at[y], y_dev(at_y(k))) for k in AROUND}
    with scope("s_gp"):
        arrive(dw_copy, dw_recv, partner)
        dw_hat = dw_buf[c] + dw_recv[...].astype(F32)
        proto_unit, proto_inverse = unit_along(proto_ref[...], 0)
        gp_ref[...] = (
            (total_cols / math.sqrt(total_rows))
            * proto_inverse
            * (dw_hat - proto_unit * jnp.sum(proto_unit * dw_hat, axis=0, keepdims=True))
        )
    with scope("s_lossz"):
        lse = jnp.log(stud_total)
        part = lse[:, 0:128]
        for lane in range(128, rows, 128):
            part = part + lse[:, lane : lane + 128]
        loss_x[c] = part - finish_z(z_loss, loss_z)
        loss_copy = send(loss_x.at[c], loss_x.at[c], partner)
    with scope("s_gathery"):
        for k in AROUND:
            source = at_y(NY - k)
            arrive(gather_y[k], ygather.at[source], y_dev(source))
    with scope("s_dz"):
        for i in range(NY):
            for q in range(NZ):
                r = 16 * (q // 2)
                s = half_own * (q % 2)
                base = i * piece + r if r < piece else half_k + i * piece + r - piece
                dzt[base : base + 16, s : s + half_own] = ygather[i, q].astype(F32)
        dz = jnp.transpose(dzt[...])
        stud_unit, stud_inverse = unit_along(stud_ref[...], 1)
        gs_ref[...] = stud_inverse * (
            dz - stud_unit * jnp.sum(stud_unit * dz, axis=1, keepdims=True)
        )
    with scope("s_end"):
        arrive(loss_copy, loss_x.at[1 - c], partner)
        loss_ref[...] = jnp.broadcast_to(
            jnp.sum(loss_x[0] + loss_x[1], axis=1, keepdims=True) / total_rows, loss_ref.shape
        )
        for copy in started:
            copy.wait_send()


def solution(mesh):
    def shards(teacher_emb, student_emb, prototypes):
        own, k_dim = teacher_emb.shape
        cols = prototypes.shape[1]
        rows, both = NX * own, 2 * cols
        total_rows = own * mesh.shape["dp"]
        total_cols = cols * mesh.shape["dp"] * mesh.shape["proto"]
        vmem = pltpu.VMEM
        piece = k_dim // 8
        scratch = [
            vmem((NX, 4, k_dim // 4, own), BF16),
            vmem((NX, 4, k_dim // 4, own), BF16),
            vmem((NC, k_dim, cols), BF16),
            vmem((NC, cols, k_dim), BF16),
            vmem((k_dim + 16, both), BF16),
            vmem((NX, both, own), BF16),
            vmem((NX, both, own), BF16),
            vmem((both, 128), F32),
            vmem((ITERS, NC, 1, both), F32),
            vmem((ITERS + 1, NX * NY, 1, rows), F32),
            vmem((ITERS + 1, NZ, 1, rows), F32),
            vmem((NX * NY, 1, 128), F32),
            vmem((NZ, 1, 128), F32),
            vmem((2, NX, k_dim // 2, own), BF16),
            vmem((2, NY, NX, piece, own), BF16),
            vmem((2, NX, k_dim // 2, own), BF16),
            vmem((2, NY, NX, piece, own), BF16),
            vmem((2, NY, piece, own), BF16),
            vmem((2, NX, piece, own), BF16),
            vmem((2, NY, piece, own), BF16),
            vmem((2, NX, piece, own), BF16),
            vmem((2, NZ, 16, own // 2), BF16),
            vmem((2, NZ, 16, own // 2), BF16),
            vmem((NY, NZ, 16, own // 2), BF16),
            vmem((NX, 1, own), F32),
            vmem((2, 2 * NX, 1, own // 2), F32),
            vmem((2, k_dim, cols), F32),
            vmem((k_dim, cols), BF16),
            vmem((k_dim, cols), BF16),
            vmem((2, 1, 128), F32),
            vmem((k_dim, own), F32),
            pltpu.SemaphoreType.DMA((240,)),
            pltpu.SemaphoreType.DMA((240,)),
        ]
        loss, grad_student, grad_prototypes = pl.pallas_call(
            functools.partial(kernel, float(total_rows), float(total_cols)),
            out_shape=(
                jax.ShapeDtypeStruct((1, 128), F32),
                jax.ShapeDtypeStruct((own, k_dim), F32),
                jax.ShapeDtypeStruct((k_dim, cols), F32),
            ),
            in_specs=[pl.BlockSpec(memory_space=vmem)] * 3,
            out_specs=[pl.BlockSpec(memory_space=vmem)] * 3,
            scratch_shapes=scratch,
            compiler_params=pltpu.CompilerParams(
                collective_id=0, has_side_effects=True, vmem_limit_bytes=60 << 20
            ),
            name="prototype_head",
        )(teacher_emb, student_emb, prototypes)
        return loss[0, 0], grad_student, grad_prototypes

    in_specs = (P("dp", None), P("dp", None), P(None, ("dp", "proto")))
    out_specs = (P(), P("dp", None), P(None, ("dp", "proto")))
    return jax.shard_map(shards, mesh=mesh, in_specs=in_specs, out_specs=out_specs, check_vma=False)
```

```python
import functools
import math

import jax
import jax.numpy as jnp
from jax import lax
from jax.experimental import pallas as pl
from jax.experimental.pallas import tpu as pltpu
from jax.sharding import PartitionSpec as P

ITERS = 3
TEACHER_TEMP = 0.04
STUDENT_TEMP = 0.1
NORM_EPS = 1e-06
LOG2E = 1.4426950408889634
NX, NC, NY, NZ = 4, 2, 4, 8
GROUPS = 43

MESH = pl.DeviceIdType.MESH
scope = jax.named_scope
F32, BF16 = jnp.float32, jnp.bfloat16
NT = (((1,), (1,)), ((), ()))


def unit_along(values, axis):
    floats = values.astype(F32)
    inverse = lax.rsqrt(jnp.sum(floats * floats, axis=axis, keepdims=True) + NORM_EPS)
    return floats * inverse, inverse


def split_rows(vec):
    n = vec.shape[1]
    high = vec.astype(BF16).astype(F32)
    low = vec - high
    row = lax.broadcasted_iota(jnp.int32, (16, n), 0)
    both = jnp.where(row == 0, high, jnp.where(row == 1, low, 0.0))
    return both.astype(BF16)


def kernel(
    total_rows,
    total_cols,
    teach_hbm,
    stud_hbm,
    proto_hbm,
    loss_ref,
    gs_ref,
    gp_ref,
    teach_ref,
    stud_ref,
    proto_ref,
    teach_all,
    stud_all,
    proto_all,
    protot_all,
    left,
    exp_t,
    exp_n,
    exp_s,
    acc,
    colx,
    xy_vec,
    z_vec,
    xy_loss,
    z_loss,
    send_a,
    send_b,
    recv_a,
    recv_b,
    send_a2,
    send_b2,
    recv_a2,
    recv_b2,
    zsend,
    zrecv,
    ygather,
    cross,
    fac_mix,
    dw_buf,
    dw_send,
    dw_recv,
    loss_x,
    dzt,
    ssem,
    rsem,
    lsem,
):
    d = lax.axis_index("dp")
    p = lax.axis_index("proto")
    x, c = d // NC, lax.rem(d, NC)
    z, y = p // NY, lax.rem(p, NY)
    own = teach_ref.shape[0]
    k_dim, cols = proto_ref.shape
    rows = NX * own
    both_cols = 2 * cols
    half_own = own // 2

    def at_x(k):
        return lax.rem(x + k, NX)

    def at_y(k):
        return lax.rem(y + k, NY)

    def at_z(k):
        return lax.rem(z + k, NZ)

    def dev(xx, cc, yy, zz):
        return (xx * NC + cc, zz * NY + yy)

    def x_dev(xx):
        return dev(xx, c, y, z)

    def y_dev(yy):
        return dev(x, c, yy, z)

    def z_dev(zz):
        return dev(x, c, y, zz)

    partner = dev(x, 1 - c, y, z)
    xy_peers = [dev(at_x(k // 4), c, at_y(k % 4), z) for k in range(1, 16)]
    z_peers = [z_dev(at_z(k)) for k in range(1, 8)]
    everyone = [partner] + xy_peers + z_peers
    AROUND = (2, 1, 3)

    barrier = pltpu.get_barrier_semaphore()
    for peer in everyone:
        pl.semaphore_signal(barrier, inc=1, device_id=peer, device_id_type=MESH)

    groups = []

    def group(span):
        groups.append(span)
        return len(groups) - 1

    def copy_of(g, src, dst, peer):
        return pltpu.make_async_remote_copy(
            src_ref=src,
            dst_ref=dst,
            send_sem=ssem.at[g],
            recv_sem=rsem.at[g],
            device_id=peer,
            device_id_type=MESH,
        )

    def send(g, src, dst, peer):
        copy_of(g, src, dst, peer).start()

    def send_one(src, dst, peer):
        g = group(src)
        send(g, src, dst, peer)
        return g

    def arrive(g):
        copy_of(g, groups[g], groups[g], partner).wait_recv()

    def local(src, dst, sem):
        copy = pltpu.make_async_copy(src, dst, lsem.at[sem])
        copy.start()
        return copy

    quarter = own // 4

    def put_own(blocks, hat):
        hat_t = jnp.transpose(hat).astype(BF16)
        for q in range(4):
            blocks[x, q] = hat_t[:, q * quarter : (q + 1) * quarter]

    def start_gather(blocks):
        far = send_one(blocks.at[x, y], blocks.at[x, y], x_dev(at_x(2)))
        near = {}
        for k in (1, 3):
            near[k] = send_one(blocks.at[x, y], blocks.at[x, y], x_dev(at_x(k)))
        rest = []
        for t in (1, 2):
            rest.append(group(blocks.at[0, pl.ds(0, 2)]))
            for k in (1, 3):
                q = at_y(t)
                send(rest[-1], blocks.at[x, q], blocks.at[x, q], x_dev(at_x(k)))
        return far, near, *rest

    def relay_far(blocks, copies):
        source = at_x(2)
        arrive(copies[0])
        g = group(blocks.at[0, pl.ds(0, 3)])
        for k in AROUND:
            send(g, blocks.at[source, y], blocks.at[source, y], y_dev(at_y(k)))
        return g

    def relay_near(blocks, copies):
        g = group(blocks.at[0, pl.ds(0, 2)])
        for k in (1, 3):
            source = at_x(NX - k)
            arrive(copies[1][k])
            send(g, blocks.at[source, y], blocks.at[source, y], y_dev(at_y(1)))
        return g

    def block_of(blocks, j):
        return jnp.concatenate([blocks[j, q] for q in range(4)], axis=1)

    def pair_of(blocks, j, pair):
        return jnp.concatenate([blocks[j, q] for q in pair], axis=1)

    with scope("s_load"):
        teach_load = local(teach_hbm, teach_ref, 0)
        proto_load = local(proto_hbm, proto_ref, 1)
        stud_load = local(stud_hbm, stud_ref, 2)
        teach_load.wait()
    with scope("s_norm"):
        put_own(teach_all, unit_along(teach_ref[...], 1)[0])
    with scope("s_barrier"):
        pl.semaphore_wait(barrier, len(everyone))
    with scope("s_norm"):
        teach_copies = start_gather(teach_all)
        proto_load.wait()
        proto_unit = unit_along(proto_ref[...], 0)[0]
        protot_all[c] = jnp.transpose(proto_unit).astype(BF16)
        protot_copy = send_one(protot_all.at[c], protot_all.at[c], partner)
        proto_all[c] = proto_unit.astype(BF16)
        proto_copy = send_one(proto_all.at[c], proto_all.at[c], partner)
        stud_load.wait()
        put_own(stud_all, unit_along(stud_ref[...], 1)[0])
        stud_copies = start_gather(stud_all)

    def lanes_of(q):
        start = q * quarter
        return pl.ds(start if isinstance(q, int) else pl.multiple_of(start, quarter), quarter)

    def teacher_part(block, pair, half=None):
        if half is None:
            protos_t, rows_out = protot_all[...].reshape(both_cols, k_dim), slice(None)
        else:
            protos_t = protot_all[half]
            rows_out = pl.ds(pl.multiple_of(half * cols, cols), cols)
        prod = jnp.dot(protos_t, pair_of(teach_all, block, pair), preferred_element_type=F32)
        e = jnp.exp2(prod * (LOG2E / TEACHER_TEMP))
        low = e.astype(BF16)
        for i, q in enumerate(pair):
            exp_t[block, rows_out, lanes_of(q)] = low[:, i * quarter : (i + 1) * quarter]
        part = e[:, 0:128]
        for lane in range(128, half_own, 128):
            part = part + e[:, lane : lane + 128]
        acc[rows_out, :] += part

    def student_block(block):
        for pair in ((0, 1), (2, 3)):
            prod = jnp.dot(
                protot_all[...].reshape(both_cols, k_dim),
                pair_of(stud_all, block, pair),
                preferred_element_type=F32,
            )
            low = jnp.exp2(prod * (LOG2E / STUDENT_TEMP)).astype(BF16)
            exp_s[block, :, pair[0] * quarter : (pair[1] + 1) * quarter] = low

    with scope("s_T_own"):
        acc[...] = jnp.zeros_like(acc)
        teacher_part(x, (0, 1), c)
        teacher_part(x, (2, 3), c)
        arrive(protot_copy)
        teacher_part(x, (0, 1), 1 - c)
        teacher_part(x, (2, 3), 1 - c)
    with scope("s_relay_far"):
        teach_far = relay_far(teach_all, teach_copies)
    with scope("s_relay_near"):
        teach_near = relay_near(teach_all, teach_copies)
    with scope("s_direct"):
        arrive(teach_copies[2])
    with scope("s_T_early"):
        for k in (1, 3):
            teacher_part(at_x(k), (y, at_y(1)))
    with scope("s_direct"):
        arrive(teach_copies[3])
    with scope("s_relay_wait"):
        arrive(teach_near)
    with scope("s_T_late"):
        for k in (1, 3):
            teacher_part(at_x(k), (at_y(2), at_y(3)))
    with scope("s_far_wait"):
        arrive(teach_far)
    with scope("s_T_far"):
        teacher_part(at_x(2), (0, 1))
        teacher_part(at_x(2), (2, 3))
    with scope("s_stud_relay"):
        stud_far = relay_far(stud_all, stud_copies)
        stud_near = relay_near(stud_all, stud_copies)

    def column_scale(step, sums):
        colx[step, c] = sums
        arrive(send_one(colx.at[step, c], colx.at[step, c], partner))
        return 1.0 / (total_cols * (colx[step, 0] + colx[step, 1]))

    def first_column_sums():
        parts = []
        for b in range(both_cols // 128):
            t = jnp.transpose(acc[b * 128 : (b + 1) * 128, :])
            parts.append(jnp.sum(t, axis=0, keepdims=True))
        return jnp.concatenate(parts, axis=1)

    def column_sums(row_scale):
        both = split_rows(row_scale)
        total = None
        for j in range(NX):
            part = jnp.dot(
                both[:, j * own : (j + 1) * own], exp_n[j], preferred_element_type=F32
            )
            total = part if total is None else total + part
        return total[0:1] + total[1:2]

    def row_sums(col_scale):
        both = split_rows(col_scale)
        parts = []
        for j in range(NX):
            part = jnp.dot(both, exp_t[j], preferred_element_type=F32)
            parts.append(part[0:1] + part[1:2])
        return jnp.concatenate(parts, axis=1)

    xy_me = x * NY + y

    def send_xy(buf):
        g = group(buf.at[pl.ds(0, 15)])
        for peer in xy_peers:
            send(g, buf.at[xy_me], buf.at[xy_me], peer)
        return g

    def start_xy(buf, vec):
        buf[xy_me] = vec
        return send_xy(buf)

    def start_z(buf, vec):
        buf[z] = vec
        g = group(buf.at[pl.ds(0, 7)])
        for peer in z_peers:
            send(g, buf.at[z], buf.at[z], peer)
        return g

    def finish(buf, g):
        arrive(g)
        total = buf[0]
        for i in range(1, buf.shape[0]):
            total = total + buf[i]
        return total

    half_k, piece = k_dim // 2, k_dim // 8

    def put_block(which, j, value):
        low = value.astype(BF16)
        send_a[which, j] = low[:half_k]
        for q in range(NY):
            send_b[which, q, j] = low[half_k + q * piece : half_k + (q + 1) * piece]

    def first_groups(which):
        return (
            group(recv_a.at[which, pl.ds(0, 3)]),
            group(recv_b.at[which, pl.ds(0, 3)]),
        )

    def send_block(which, first, k):
        j = at_x(k)
        if k:
            send(first[0], send_a.at[which, j], recv_a.at[which, x], x_dev(j))
        for h in AROUND:
            send(
                first[1], send_b.at[which, at_y(h), j], recv_b.at[which, y, j], y_dev(at_y(h))
            )

    def start_second(which, first):
        recv_a[which, x] = send_a[which, x]
        recv_b[which, y] = send_b[which, y]
        arrive(first[0])
        total = recv_a[which, 0].astype(F32)
        for i in range(1, NX):
            total = total + recv_a[which, i].astype(F32)
        low = total.astype(BF16)
        for q in range(NY):
            send_a2[which, q] = low[q * piece : (q + 1) * piece]
        a2 = group(recv_a2.at[which, pl.ds(0, 3)])
        for k in AROUND:
            send(a2, send_a2.at[which, at_y(k)], recv_a2.at[which, y], y_dev(at_y(k)))
        arrive(first[1])
        for j in range(NX):
            total = recv_b[which, 0, j].astype(F32)
            for i in range(1, NY):
                total = total + recv_b[which, i, j].astype(F32)
            send_b2[which, j] = total.astype(BF16)
        b2 = group(recv_b2.at[which, pl.ds(0, 3)])
        for k in AROUND:
            send(b2, send_b2.at[which, at_x(k)], recv_b2.at[which, x], x_dev(at_x(k)))
        return a2, b2

    def start_third(which, second):
        a2, b2 = second
        recv_a2[which, y] = send_a2[which, y]
        recv_b2[which, x] = send_b2[which, x]
        arrive(a2)
        arrive(b2)
        low = recv_a2[which, 0].astype(F32)
        high = recv_b2[which, 0].astype(F32)
        for i in range(1, 4):
            low = low + recv_a2[which, i].astype(F32)
            high = high + recv_b2[which, i].astype(F32)
        low, high = low.astype(BF16), high.astype(BF16)
        for q in range(NZ):
            r = 16 * (q // 2)
            s = half_own * (q % 2)
            part = low[r : r + 16] if r < piece else high[r - piece : r - piece + 16]
            zsend[which, q] = part[:, s : s + half_own]
        third = group(zrecv.at[which, pl.ds(0, 7)])
        for k in range(1, NZ):
            send(third, zsend.at[which, at_z(k)], zrecv.at[which, z], z_dev(at_z(k)))
        return third

    def finish_third(which, third):
        zrecv[which, z] = zsend[which, z]
        arrive(third)
        total = zrecv[which, 0].astype(F32)
        for i in range(1, NZ):
            total = total + zrecv[which, i].astype(F32)
        return total

    with scope("s_col1"):
        scale = column_scale(0, first_column_sums())
    with scope("s_row1"):
        xy_copies = start_xy(xy_vec.at[0], row_sums(scale))
    with scope("s_S_own"):
        student_block(x)
    with scope("s_transpose"):
        for j in range(NX):
            for b in range(both_cols // 128):
                for a in range(own // 128):
                    exp_n[j, a * 128 : (a + 1) * 128, b * 128 : (b + 1) * 128] = jnp.transpose(
                        exp_t[j, b * 128 : (b + 1) * 128, a * 128 : (a + 1) * 128]
                    )
    with scope("s_xy1"):
        z_copies = start_z(z_vec.at[0], finish(xy_vec.at[0], xy_copies))
    with scope("s_stud_wait"):
        arrive(stud_copies[2])
        arrive(stud_copies[3])
        arrive(stud_near)
    with scope("s_S_near"):
        for k in (1, 3):
            student_block(at_x(k))
    with scope("s_S_far"):
        arrive(stud_far)
        student_block(at_x(2))
    with scope("s_P1"):
        arrive(proto_copy)
        left[0:k_dim, 0:cols] = proto_all[0]
        left[0:k_dim, cols:] = proto_all[1]
        left[k_dim:, :] = jnp.ones((16, both_cols), BF16)
        stud_sums = []
        for j in range(NX):
            value = jnp.dot(left[...], exp_s[j], preferred_element_type=F32)
            put_block(0, j, value[0:k_dim])
            stud_sums.append(value[k_dim : k_dim + 1])
        stud_xy = start_xy(xy_vec.at[3], jnp.concatenate(stud_sums, axis=1))
    with scope("s_z1"):
        row_scale = 1.0 / (total_rows * finish(z_vec.at[0], z_copies))

    with scope("s_col2"):
        sums = column_sums(row_scale)
    with scope("s_colx2"):
        scale = column_scale(1, sums)
    with scope("s_row2"):
        xy_copies = start_xy(xy_vec.at[1], row_sums(scale))
        first1 = first_groups(0)
        for k in (2, 1, 3, 0):
            send_block(0, first1, k)
    with scope("s_studxy"):
        stud_z = start_z(z_vec.at[3], finish(xy_vec.at[3], stud_xy))
    with scope("s_xy2"):
        z_copies = start_z(z_vec.at[1], finish(xy_vec.at[1], xy_copies))
    with scope("s_second1"):
        second1 = start_second(0, first1)
    with scope("s_z2"):
        row_scale = 1.0 / (total_rows * finish(z_vec.at[1], z_copies))

    with scope("s_col3"):
        sums = column_sums(row_scale)
    with scope("s_colx3"):
        scale = column_scale(2, sums)
    with scope("s_P2"):
        for h in range(NC):
            left[0:k_dim, h * cols : (h + 1) * cols] = (
                proto_all[h].astype(F32) * scale[:, h * cols : (h + 1) * cols]
            ).astype(BF16)
        left[k_dim:, :] = split_rows(scale)
        first2 = first_groups(1)
        for k in (2, 1, 3, 0):
            j = at_x(k)
            value = jnp.dot(left[...], exp_t[j], preferred_element_type=F32)
            put_block(1, j, value[0:k_dim])
            send_block(1, first2, k)
            xy_vec[2, xy_me, :, pl.ds(pl.multiple_of(j * own, own), own)] = (
                value[k_dim : k_dim + 1] + value[k_dim + 1 : k_dim + 2]
            )
            cross[j] = jnp.sum(
                value[0:k_dim] * block_of(stud_all, j).astype(F32), axis=0, keepdims=True
            )
        xy_copies = send_xy(xy_vec.at[2])
    with scope("s_third1"):
        third1 = start_third(0, second1)

    with scope("s_dwS"):
        stud_total = finish(z_vec.at[3], stud_z)
        stud_factor = (1.0 / STUDENT_TEMP) / stud_total
        for h in range(NC):
            total = None
            for j in range(NX):
                weights = (
                    block_of(stud_all, j).astype(F32) * stud_factor[:, j * own : (j + 1) * own]
                ).astype(BF16)
                part = lax.dot_general(
                    weights,
                    exp_s[j, h * cols : (h + 1) * cols, :],
                    NT,
                    preferred_element_type=F32,
                )
                total = part if total is None else total + part
            dw_buf[h] = total
    with scope("s_second2"):
        second2 = start_second(1, first2)
    with scope("s_xy3"):
        z_copies = start_z(z_vec.at[2], finish(xy_vec.at[2], xy_copies))
    with scope("s_third2"):
        third2 = start_third(1, second2)
    with scope("s_z3"):
        row_scale = 1.0 / (total_rows * finish(z_vec.at[2], z_copies))
        teach_factor = (total_rows / STUDENT_TEMP) * row_scale

    with scope("s_loss"):
        part = None
        for j in range(NX):
            term = teach_factor[:, j * own : (j + 1) * own] * cross[j]
            for lane in range(0, own, 128):
                t = term[:, lane : lane + 128]
                part = t if part is None else part + t
        loss_xy = start_xy(xy_loss, part)

    with scope("s_mix"):
        part1 = finish_third(0, third1)
        part2 = finish_third(1, third2)
        for i in range(2 * NX):
            s = i * half_own
            fac_mix[0, i] = stud_factor[:, s : s + half_own]
            fac_mix[1, i] = teach_factor[:, s : s + half_own]
        mine = x * 2 + lax.rem(z, 2)
        ygather[y, z] = (fac_mix[0, mine] * part1 - fac_mix[1, mine] * part2).astype(BF16)
        gather_z = group(ygather.at[0, pl.ds(0, 7)])
        for k in range(1, NZ):
            send(gather_z, ygather.at[y, z], ygather.at[y, z], z_dev(at_z(k)))

    with scope("s_dwT"):
        for h in range(NC):
            total = None
            for j in range(NX):
                weights = (
                    block_of(stud_all, j).astype(F32) * teach_factor[:, j * own : (j + 1) * own]
                ).astype(BF16)
                part = lax.dot_general(
                    weights,
                    exp_t[j, h * cols : (h + 1) * cols, :],
                    NT,
                    preferred_element_type=F32,
                )
                total = part if total is None else total + part
            dw_buf[h] = dw_buf[h] - total * scale[:, h * cols : (h + 1) * cols]
        dw_send[...] = dw_buf[1 - c].astype(BF16)
        dw_copy = send_one(dw_send, dw_recv, partner)
    with scope("s_lossxy"):
        loss_z = start_z(z_loss, finish(xy_loss, loss_xy))
    with scope("s_gatherz"):
        arrive(gather_z)
        gather_y = group(ygather.at[pl.ds(0, 3)])
        for k in AROUND:
            send(gather_y, ygather.at[y], ygather.at[y], y_dev(at_y(k)))
    with scope("s_gp"):
        arrive(dw_copy)
        dw_hat = dw_buf[c] + dw_recv[...].astype(F32)
        proto_unit, proto_inverse = unit_along(proto_ref[...], 0)
        gp_ref[...] = (
            (total_cols / math.sqrt(total_rows))
            * proto_inverse
            * (dw_hat - proto_unit * jnp.sum(proto_unit * dw_hat, axis=0, keepdims=True))
        )
    with scope("s_lossz"):
        lse = jnp.log(stud_total)
        part = lse[:, 0:128]
        for lane in range(128, rows, 128):
            part = part + lse[:, lane : lane + 128]
        loss_x[c] = part - finish(z_loss, loss_z)
        loss_copy = send_one(loss_x.at[c], loss_x.at[c], partner)
    def sent(some):
        for g in some:
            copy_of(g, groups[g], groups[g], partner).wait_send()

    with scope("s_sent"):
        early = [g for g in range(len(groups)) if g not in (gather_y, loss_copy)]
        sent(early)
    with scope("s_gathery"):
        arrive(gather_y)
    with scope("s_dz"):
        for i in range(NY):
            for q in range(NZ):
                r = 16 * (q // 2)
                s = half_own * (q % 2)
                base = i * piece + r if r < piece else half_k + i * piece + r - piece
                dzt[base : base + 16, s : s + half_own] = ygather[i, q].astype(F32)
        dz = jnp.transpose(dzt[...])
        stud_unit, stud_inverse = unit_along(stud_ref[...], 1)
        gs_ref[...] = stud_inverse * (
            dz - stud_unit * jnp.sum(stud_unit * dz, axis=1, keepdims=True)
        )
    with scope("s_end"):
        arrive(loss_copy)
        loss_ref[...] = jnp.broadcast_to(
            jnp.sum(loss_x[0] + loss_x[1], axis=1, keepdims=True) / total_rows, loss_ref.shape
        )
        assert len(groups) == GROUPS, len(groups)
        sent((gather_y, loss_copy))


def store_kernel(*refs):
    results, outs, sem = refs[:3], refs[3:6], refs[6]
    for i, (result, out) in enumerate(zip(results, outs)):
        pltpu.make_async_copy(result, out, sem.at[i]).start()
    for i, (result, out) in enumerate(zip(results, outs)):
        pltpu.make_async_copy(result, out, sem.at[i]).wait()


def solution(mesh):
    def shards(teacher_emb, student_emb, prototypes):
        own, k_dim = teacher_emb.shape
        cols = prototypes.shape[1]
        rows, both = NX * own, 2 * cols
        total_rows = own * mesh.shape["dp"]
        total_cols = cols * mesh.shape["dp"] * mesh.shape["proto"]
        vmem = pltpu.VMEM
        piece = k_dim // 8
        scratch = [
            vmem((own, k_dim), BF16),
            vmem((own, k_dim), BF16),
            vmem((k_dim, cols), BF16),
            vmem((NX, 4, k_dim, own // 4), BF16),
            vmem((NX, 4, k_dim, own // 4), BF16),
            vmem((NC, k_dim, cols), BF16),
            vmem((NC, cols, k_dim), BF16),
            vmem((k_dim + 16, both), BF16),
            vmem((NX, both, own), BF16),
            vmem((NX, own, both), BF16),
            vmem((NX, both, own), BF16),
            vmem((both, 128), F32),
            vmem((ITERS, NC, 1, both), F32),
            vmem((ITERS + 1, NX * NY, 1, rows), F32),
            vmem((ITERS + 1, NZ, 1, rows), F32),
            vmem((NX * NY, 1, 128), F32),
            vmem((NZ, 1, 128), F32),
            vmem((2, NX, k_dim // 2, own), BF16),
            vmem((2, NY, NX, piece, own), BF16),
            vmem((2, NX, k_dim // 2, own), BF16),
            vmem((2, NY, NX, piece, own), BF16),
            vmem((2, NY, piece, own), BF16),
            vmem((2, NX, piece, own), BF16),
            vmem((2, NY, piece, own), BF16),
            vmem((2, NX, piece, own), BF16),
            vmem((2, NZ, 16, own // 2), BF16),
            vmem((2, NZ, 16, own // 2), BF16),
            vmem((NY, NZ, 16, own // 2), BF16),
            vmem((NX, 1, own), F32),
            vmem((2, 2 * NX, 1, own // 2), F32),
            vmem((2, k_dim, cols), F32),
            vmem((k_dim, cols), BF16),
            vmem((k_dim, cols), BF16),
            vmem((2, 1, 128), F32),
            vmem((k_dim, own), F32),
            pltpu.SemaphoreType.DMA((GROUPS,)),
            pltpu.SemaphoreType.DMA((GROUPS,)),
            pltpu.SemaphoreType.DMA((3,)),
        ]
        anywhere = pl.BlockSpec(memory_space=pl.ANY)
        in_vmem = pl.BlockSpec(memory_space=vmem)
        shapes = ((1, 128), (own, k_dim), (k_dim, cols))
        results = pl.pallas_call(
            functools.partial(kernel, float(total_rows), float(total_cols)),
            out_shape=tuple(vmem(shape, F32) for shape in shapes),
            in_specs=[anywhere] * 3,
            out_specs=[in_vmem] * 3,
            scratch_shapes=scratch,
            compiler_params=pltpu.CompilerParams(
                collective_id=0, has_side_effects=True, vmem_limit_bytes=60 << 20
            ),
            name="prototype_head",
        )(teacher_emb, student_emb, prototypes)
        loss, grad_student, grad_prototypes = pl.pallas_call(
            store_kernel,
            out_shape=tuple(jax.ShapeDtypeStruct(shape, F32) for shape in shapes),
            in_specs=[in_vmem] * 3,
            out_specs=[anywhere] * 3,
            scratch_shapes=[pltpu.SemaphoreType.DMA((3,))],
            name="store_results",
        )(*(pltpu.with_memory_space_constraint(result, vmem) for result in results))
        return loss[0, 0], grad_student, grad_prototypes

    in_specs = (P("dp", None), P("dp", None), P(None, ("dp", "proto")))
    out_specs = (P(), P("dp", None), P(None, ("dp", "proto")))
    return jax.shard_map(shards, mesh=mesh, in_specs=in_specs, out_specs=out_specs, check_vma=False)
```

```python
import functools
import math

import jax
import jax.numpy as jnp
from jax import lax
from jax.experimental import pallas as pl
from jax.experimental.pallas import tpu as pltpu
from jax.sharding import PartitionSpec as P

ITERS = 3
TEACHER_TEMP = 0.04
STUDENT_TEMP = 0.1
NORM_EPS = 1e-06
LOG2E = 1.4426950408889634
NX, NC, NY, NZ = 4, 2, 4, 8
GROUPS = 42

MESH = pl.DeviceIdType.MESH
scope = jax.named_scope
F32, BF16 = jnp.float32, jnp.bfloat16
NT = (((1,), (1,)), ((), ()))


def unit_along(values, axis):
    floats = values.astype(F32)
    inverse = lax.rsqrt(jnp.sum(floats * floats, axis=axis, keepdims=True) + NORM_EPS)
    return floats * inverse, inverse


def split_rows(vec):
    n = vec.shape[1]
    high = vec.astype(BF16).astype(F32)
    low = vec - high
    row = lax.broadcasted_iota(jnp.int32, (16, n), 0)
    both = jnp.where(row == 0, high, jnp.where(row == 1, low, 0.0))
    return both.astype(BF16)


def kernel(
    total_rows,
    total_cols,
    teach_hbm,
    stud_hbm,
    proto_hbm,
    loss_ref,
    gs_ref,
    gp_ref,
    teach_ref,
    stud_ref,
    proto_ref,
    teach_all,
    stud_all,
    proto_all,
    protot_all,
    left,
    exp_t,
    exp_n,
    exp_s,
    acc,
    colx,
    xy_vec,
    z_vec,
    xy_loss,
    z_loss,
    send_a,
    send_b,
    far_a,
    far_b,
    sum_a,
    sum_b,
    recv_a,
    recv_b,
    send_a2,
    send_b2,
    recv_a2,
    recv_b2,
    zsend,
    zrecv,
    ygather,
    cross,
    fac_mix,
    dw_buf,
    dw_send,
    dw_recv,
    loss_x,
    dzt,
    ssem,
    rsem,
    lsem,
):
    d = lax.axis_index("dp")
    p = lax.axis_index("proto")
    x, c = d // NC, lax.rem(d, NC)
    z, y = p // NY, lax.rem(p, NY)
    own = teach_ref.shape[0]
    k_dim, cols = proto_ref.shape
    rows = NX * own
    both_cols = 2 * cols
    half_own = own // 2

    def at_x(k):
        return lax.rem(x + k, NX)

    def at_y(k):
        return lax.rem(y + k, NY)

    def at_z(k):
        return lax.rem(z + k, NZ)

    def dev(xx, cc, yy, zz):
        return (xx * NC + cc, zz * NY + yy)

    def x_dev(xx):
        return dev(xx, c, y, z)

    def y_dev(yy):
        return dev(x, c, yy, z)

    def z_dev(zz):
        return dev(x, c, y, zz)

    partner = dev(x, 1 - c, y, z)
    xy_peers = [dev(at_x(k // 4), c, at_y(k % 4), z) for k in range(1, 16)]
    z_peers = [z_dev(at_z(k)) for k in range(1, 8)]
    everyone = [partner] + xy_peers + z_peers
    AROUND = (2, 1, 3)

    barrier = pltpu.get_barrier_semaphore()
    for peer in everyone:
        pl.semaphore_signal(barrier, inc=1, device_id=peer, device_id_type=MESH)

    groups = []

    def group(span):
        groups.append(span)
        return len(groups) - 1

    def copy_of(g, src, dst, peer):
        return pltpu.make_async_remote_copy(
            src_ref=src,
            dst_ref=dst,
            send_sem=ssem.at[g],
            recv_sem=rsem.at[g],
            device_id=peer,
            device_id_type=MESH,
        )

    def send(g, src, dst, peer):
        copy_of(g, src, dst, peer).start()

    def send_one(src, dst, peer):
        g = group(src)
        send(g, src, dst, peer)
        return g

    def arrive(g):
        copy_of(g, groups[g], groups[g], partner).wait_recv()

    def local(src, dst, sem):
        copy = pltpu.make_async_copy(src, dst, lsem.at[sem])
        copy.start()
        return copy

    quarter = own // 4

    def put_own(blocks, hat):
        hat_t = jnp.transpose(hat).astype(BF16)
        for q in range(4):
            blocks[x, q] = hat_t[:, q * quarter : (q + 1) * quarter]

    def start_gather(blocks):
        far = send_one(blocks.at[x, y], blocks.at[x, y], x_dev(at_x(2)))
        near = []
        for pair in ((0, 1), (2, 3)):
            near.append(group(blocks.at[0, pl.ds(0, 4)]))
            for t in pair:
                for k in (1, 3):
                    q = at_y(t)
                    send(near[-1], blocks.at[x, q], blocks.at[x, q], x_dev(at_x(k)))
        return far, *near

    def relay_far(blocks, copies):
        source = at_x(2)
        arrive(copies[0])
        g = group(blocks.at[0, pl.ds(0, 3)])
        for k in AROUND:
            send(g, blocks.at[source, y], blocks.at[source, y], y_dev(at_y(k)))
        return g

    def block_of(blocks, j):
        return jnp.concatenate([blocks[j, q] for q in range(4)], axis=1)

    def pair_of(blocks, j, pair):
        return jnp.concatenate([blocks[j, q] for q in pair], axis=1)

    with scope("s_load"):
        teach_load = local(teach_hbm, teach_ref, 0)
        proto_load = local(proto_hbm, proto_ref, 1)
        stud_load = local(stud_hbm, stud_ref, 2)
        teach_load.wait()
    with scope("s_norm"):
        put_own(teach_all, unit_along(teach_ref[...], 1)[0])
    with scope("s_barrier"):
        pl.semaphore_wait(barrier, len(everyone))
    with scope("s_norm"):
        teach_copies = start_gather(teach_all)
        proto_load.wait()
        proto_unit = unit_along(proto_ref[...], 0)[0]
        protot_all[c] = jnp.transpose(proto_unit).astype(BF16)
        protot_copy = send_one(protot_all.at[c], protot_all.at[c], partner)
        proto_all[c] = proto_unit.astype(BF16)
        proto_copy = send_one(proto_all.at[c], proto_all.at[c], partner)
        stud_load.wait()
        put_own(stud_all, unit_along(stud_ref[...], 1)[0])
        stud_copies = start_gather(stud_all)

    def lanes_of(q):
        start = q * quarter
        return pl.ds(start if isinstance(q, int) else pl.multiple_of(start, quarter), quarter)

    def teacher_part(block, pair, half=None):
        if half is None:
            protos_t, rows_out = protot_all[...].reshape(both_cols, k_dim), slice(None)
        else:
            protos_t = protot_all[half]
            rows_out = pl.ds(pl.multiple_of(half * cols, cols), cols)
        prod = jnp.dot(protos_t, pair_of(teach_all, block, pair), preferred_element_type=F32)
        e = jnp.exp2(prod * (LOG2E / TEACHER_TEMP))
        low = e.astype(BF16)
        for i, q in enumerate(pair):
            exp_t[block, rows_out, lanes_of(q)] = low[:, i * quarter : (i + 1) * quarter]
        part = e[:, 0:128]
        for lane in range(128, half_own, 128):
            part = part + e[:, lane : lane + 128]
        acc[rows_out, :] += part

    def student_block(block):
        for pair in ((0, 1), (2, 3)):
            prod = jnp.dot(
                protot_all[...].reshape(both_cols, k_dim),
                pair_of(stud_all, block, pair),
                preferred_element_type=F32,
            )
            low = jnp.exp2(prod * (LOG2E / STUDENT_TEMP)).astype(BF16)
            exp_s[block, :, pair[0] * quarter : (pair[1] + 1) * quarter] = low

    with scope("s_T_own"):
        acc[...] = jnp.zeros_like(acc)
        teacher_part(x, (0, 1), c)
        teacher_part(x, (2, 3), c)
        arrive(protot_copy)
        teacher_part(x, (0, 1), 1 - c)
        teacher_part(x, (2, 3), 1 - c)
    with scope("s_relay_far"):
        teach_far = relay_far(teach_all, teach_copies)
    with scope("s_direct"):
        arrive(teach_copies[1])
    with scope("s_T_early"):
        for k in (1, 3):
            teacher_part(at_x(k), (y, at_y(1)))
    with scope("s_direct"):
        arrive(teach_copies[2])
    with scope("s_T_late"):
        for k in (1, 3):
            teacher_part(at_x(k), (at_y(2), at_y(3)))
    with scope("s_far_wait"):
        arrive(teach_far)
    with scope("s_T_far"):
        teacher_part(at_x(2), (0, 1))
        teacher_part(at_x(2), (2, 3))
    with scope("s_stud_relay"):
        stud_far = relay_far(stud_all, stud_copies)

    def start_column_scale(step, sums):
        colx[step, c] = sums
        return send_one(colx.at[step, c], colx.at[step, c], partner)

    def finish_column_scale(step, g):
        arrive(g)
        return 1.0 / (total_cols * (colx[step, 0] + colx[step, 1]))

    def column_scale(step, sums):
        return finish_column_scale(step, start_column_scale(step, sums))

    def first_column_sums():
        parts = []
        for b in range(both_cols // 128):
            t = jnp.transpose(acc[b * 128 : (b + 1) * 128, :])
            parts.append(jnp.sum(t, axis=0, keepdims=True))
        return jnp.concatenate(parts, axis=1)

    def column_sums(row_scale):
        both = split_rows(row_scale)
        total = None
        for j in range(NX):
            part = jnp.dot(
                both[:, j * own : (j + 1) * own], exp_n[j], preferred_element_type=F32
            )
            total = part if total is None else total + part
        return total[0:1] + total[1:2]

    def row_sums(col_scale):
        both = split_rows(col_scale)
        parts = []
        for j in range(NX):
            part = jnp.dot(both, exp_t[j], preferred_element_type=F32)
            parts.append(part[0:1] + part[1:2])
        return jnp.concatenate(parts, axis=1)

    xy_me = x * NY + y

    def send_xy(buf):
        g = group(buf.at[pl.ds(0, 15)])
        for peer in xy_peers:
            send(g, buf.at[xy_me], buf.at[xy_me], peer)
        return g

    def start_xy(buf, vec):
        buf[xy_me] = vec
        return send_xy(buf)

    def send_z(buf):
        g = group(buf.at[pl.ds(0, 7)])
        for peer in z_peers:
            send(g, buf.at[z], buf.at[z], peer)
        return g

    def start_z(buf, vec):
        buf[z] = vec
        return send_z(buf)

    def finish(buf, g):
        arrive(g)
        total = buf[0]
        for i in range(1, buf.shape[0]):
            total = total + buf[i]
        return total

    half_k, piece = k_dim // 2, k_dim // 8

    def put_block(which, j, value):
        low = value.astype(BF16)
        for h in range(2):
            send_a[which, j, h] = low[h * half_k // 2 : (h + 1) * half_k // 2]
        for q in range(NY):
            for h in range(2):
                r = half_k + q * piece + h * piece // 2
                send_b[which, q, h, j] = low[r : r + piece // 2]

    def first_groups(which):
        refs = (far_a, recv_a, far_b, recv_b)
        return [group(ref.at[which]) for ref in refs]

    def send_block(which, first, k):
        j = at_x(k)
        if k == 2:
            send(first[0], send_a.at[which, j, 0], far_a.at[which, 0], x_dev(at_x(1)))
            send(first[0], send_a.at[which, j, 1], far_a.at[which, 1], x_dev(at_x(3)))
        if k == 1:
            send(first[1], send_a.at[which, j, 1], recv_a.at[which, 0, 1], x_dev(j))
        if k == 3:
            send(first[1], send_a.at[which, j, 0], recv_a.at[which, 1, 0], x_dev(j))
        up, down, far = at_y(1), at_y(3), at_y(2)
        send(first[2], send_b.at[which, far, 0, j], far_b.at[which, 0, j], y_dev(up))
        send(first[2], send_b.at[which, far, 1, j], far_b.at[which, 1, j], y_dev(down))
        send(first[3], send_b.at[which, up, 1, j], recv_b.at[which, 0, 1, j], y_dev(up))
        send(first[3], send_b.at[which, down, 0, j], recv_b.at[which, 1, 0, j], y_dev(down))

    def pass_on_a(which, first):
        arrive(first[0])
        for h, k in ((0, 1), (1, 3)):
            both = send_a[which, at_x(k), h].astype(F32) + far_a[which, h].astype(F32)
            sum_a[which, h] = both.astype(BF16)
            send(first[1], sum_a.at[which, h], recv_a.at[which, h, h], x_dev(at_x(k)))

    def pass_on_b(which, first):
        arrive(first[2])
        for h, k in ((0, 1), (1, 3)):
            both = send_b[which, at_y(k), h].astype(F32) + far_b[which, h].astype(F32)
            sum_b[which, h] = both.astype(BF16)
            send(first[3], sum_b.at[which, h], recv_b.at[which, h, h], y_dev(at_y(k)))

    def start_second(which, first):
        arrive(first[1])
        total = send_a[which, x].astype(F32)
        for i in range(2):
            total = total + recv_a[which, i].astype(F32)
        low = total.astype(BF16).reshape(half_k, own)
        for q in range(NY):
            send_a2[which, q] = low[q * piece : (q + 1) * piece]
        a2 = group(recv_a2.at[which, pl.ds(0, 3)])
        for k in AROUND:
            send(a2, send_a2.at[which, at_y(k)], recv_a2.at[which, y], y_dev(at_y(k)))
        arrive(first[3])
        for j in range(NX):
            total = send_b[which, y, :, j].astype(F32)
            for i in range(2):
                total = total + recv_b[which, i, :, j].astype(F32)
            send_b2[which, j] = total.astype(BF16).reshape(piece, own)
        b2 = group(recv_b2.at[which, pl.ds(0, 3)])
        for k in AROUND:
            send(b2, send_b2.at[which, at_x(k)], recv_b2.at[which, x], x_dev(at_x(k)))
        return a2, b2

    def start_third(which, second):
        a2, b2 = second
        recv_a2[which, y] = send_a2[which, y]
        recv_b2[which, x] = send_b2[which, x]
        arrive(a2)
        arrive(b2)
        low = recv_a2[which, 0].astype(F32)
        high = recv_b2[which, 0].astype(F32)
        for i in range(1, 4):
            low = low + recv_a2[which, i].astype(F32)
            high = high + recv_b2[which, i].astype(F32)
        low, high = low.astype(BF16), high.astype(BF16)
        for q in range(NZ):
            r = 16 * (q // 2)
            s = half_own * (q % 2)
            part = low[r : r + 16] if r < piece else high[r - piece : r - piece + 16]
            zsend[which, q] = part[:, s : s + half_own]
        third = group(zrecv.at[which, pl.ds(0, 7)])
        for k in range(1, NZ):
            send(third, zsend.at[which, at_z(k)], zrecv.at[which, z], z_dev(at_z(k)))
        return third

    def finish_third(which, third):
        zrecv[which, z] = zsend[which, z]
        arrive(third)
        total = zrecv[which, 0].astype(F32)
        for i in range(1, NZ):
            total = total + zrecv[which, i].astype(F32)
        return total

    with scope("s_col1"):
        scale = column_scale(0, first_column_sums())
    with scope("s_row1"):
        xy_copies = start_xy(xy_vec.at[0], row_sums(scale))
    with scope("s_S_own"):
        student_block(x)
    with scope("s_transpose"):
        for j in range(NX):
            for b in range(both_cols // 128):
                for a in range(own // 128):
                    exp_n[j, a * 128 : (a + 1) * 128, b * 128 : (b + 1) * 128] = jnp.transpose(
                        exp_t[j, b * 128 : (b + 1) * 128, a * 128 : (a + 1) * 128]
                    )
    with scope("s_stud_wait"):
        arrive(stud_copies[1])
        arrive(stud_copies[2])
        student_block(at_x(1))
    with scope("s_xy1"):
        z_copies = start_z(z_vec.at[0], finish(xy_vec.at[0], xy_copies))
    with scope("s_S_near"):
        student_block(at_x(3))
    with scope("s_S_far"):
        arrive(stud_far)
        student_block(at_x(2))
    with scope("s_P1"):
        arrive(proto_copy)
        left[0:k_dim, 0:cols] = proto_all[0]
        left[0:k_dim, cols:] = proto_all[1]
        left[k_dim:, :] = jnp.ones((16, both_cols), BF16)
        stud_sums = []
        for j in range(NX):
            value = jnp.dot(left[...], exp_s[j], preferred_element_type=F32)
            put_block(0, j, value[0:k_dim])
            stud_sums.append(value[k_dim : k_dim + 1])
        stud_xy = start_xy(xy_vec.at[3], jnp.concatenate(stud_sums, axis=1))
    with scope("s_z1"):
        row_scale = 1.0 / (total_rows * finish(z_vec.at[0], z_copies))

    with scope("s_col2"):
        sums = column_sums(row_scale)
    with scope("s_colx2"):
        scale = column_scale(1, sums)
    with scope("s_row2"):
        xy_copies = start_xy(xy_vec.at[1], row_sums(scale))
        first1 = first_groups(0)
        for k in (2, 1, 3, 0):
            send_block(0, first1, k)
    with scope("s_studxy"):
        stud_z = start_z(z_vec.at[3], finish(xy_vec.at[3], stud_xy))
    with scope("s_xy2"):
        z_copies = start_z(z_vec.at[1], finish(xy_vec.at[1], xy_copies))
    with scope("s_pass1"):
        pass_on_a(0, first1)
        pass_on_b(0, first1)
    with scope("s_z2"):
        row_scale = 1.0 / (total_rows * finish(z_vec.at[1], z_copies))

    with scope("s_col3"):
        sums = column_sums(row_scale)
    with scope("s_colx3"):
        col_copy = start_column_scale(2, sums)
        second1 = start_second(0, first1)
        scale = finish_column_scale(2, col_copy)
    with scope("s_P2"):
        for h in range(NC):
            left[0:k_dim, h * cols : (h + 1) * cols] = (
                proto_all[h].astype(F32) * scale[:, h * cols : (h + 1) * cols]
            ).astype(BF16)
        left[k_dim:, :] = split_rows(scale)
        first2 = first_groups(1)
        for k in (2, 1, 3, 0):
            j = at_x(k)
            value = jnp.dot(left[...], exp_t[j], preferred_element_type=F32)
            put_block(1, j, value[0:k_dim])
            send_block(1, first2, k)
            z_vec[2, z, :, pl.ds(pl.multiple_of(j * own, own), own)] = (
                value[k_dim : k_dim + 1] + value[k_dim + 1 : k_dim + 2]
            )
            cross[j] = jnp.sum(
                value[0:k_dim] * block_of(stud_all, j).astype(F32), axis=0, keepdims=True
            )
        z_copies = send_z(z_vec.at[2])
    with scope("s_pass2a"):
        pass_on_a(1, first2)
    with scope("s_third1"):
        third1 = start_third(0, second1)
    with scope("s_pass2b"):
        pass_on_b(1, first2)

    with scope("s_second2"):
        second2 = start_second(1, first2)
    with scope("s_z3"):
        xy_copies = start_xy(xy_vec.at[2], finish(z_vec.at[2], z_copies))

    with scope("s_dwS"):
        stud_total = finish(z_vec.at[3], stud_z)
        stud_factor = (1.0 / STUDENT_TEMP) / stud_total
        for h in range(NC):
            total = None
            for j in range(NX):
                weights = (
                    block_of(stud_all, j).astype(F32) * stud_factor[:, j * own : (j + 1) * own]
                ).astype(BF16)
                part = lax.dot_general(
                    weights,
                    exp_s[j, h * cols : (h + 1) * cols, :],
                    NT,
                    preferred_element_type=F32,
                )
                total = part if total is None else total + part
            dw_buf[h] = total
    with scope("s_third2"):
        third2 = start_third(1, second2)
    with scope("s_xy3"):
        row_scale = 1.0 / (total_rows * finish(xy_vec.at[2], xy_copies))
        teach_factor = (total_rows / STUDENT_TEMP) * row_scale

    with scope("s_loss"):
        part = None
        for j in range(NX):
            term = teach_factor[:, j * own : (j + 1) * own] * cross[j]
            for lane in range(0, own, 128):
                t = term[:, lane : lane + 128]
                part = t if part is None else part + t
        loss_xy = start_xy(xy_loss, part)

    with scope("s_mix"):
        part1 = finish_third(0, third1)
        part2 = finish_third(1, third2)
        for i in range(2 * NX):
            s = i * half_own
            fac_mix[0, i] = stud_factor[:, s : s + half_own]
            fac_mix[1, i] = teach_factor[:, s : s + half_own]
        mine = x * 2 + lax.rem(z, 2)
        ygather[y, z] = (fac_mix[0, mine] * part1 - fac_mix[1, mine] * part2).astype(BF16)
        NEAR, FAR = (1, 7, 2, 6), (3, 5, 4)
        gather_near = group(ygather.at[0, pl.ds(0, len(NEAR))])
        gather_far = group(ygather.at[0, pl.ds(0, len(FAR))])
        for g, steps in ((gather_far, FAR), (gather_near, NEAR)):
            for k in steps:
                send(g, ygather.at[y, z], ygather.at[y, z], z_dev(at_z(k)))
        gather_y = group(ygather.at[pl.ds(0, 3)])

        def forward(steps):
            for k in steps:
                sz = at_z(k)
                for h in AROUND:
                    send(gather_y, ygather.at[y, sz], ygather.at[y, sz], y_dev(at_y(h)))

    def teacher_half(h):
        total = None
        for j in range(NX):
            weights = (
                block_of(stud_all, j).astype(F32) * teach_factor[:, j * own : (j + 1) * own]
            ).astype(BF16)
            part = lax.dot_general(
                weights,
                exp_t[j, h * cols : (h + 1) * cols, :],
                NT,
                preferred_element_type=F32,
            )
            total = part if total is None else total + part
        dw_buf[h] = dw_buf[h] - total * scale[:, h * cols : (h + 1) * cols]

    with scope("s_dwT"):
        teacher_half(0)
    with scope("s_lossxy"):
        loss_z = start_z(z_loss, finish(xy_loss, loss_xy))
    with scope("s_dwT"):
        teacher_half(1)
        dw_send[...] = dw_buf[1 - c].astype(BF16)
        dw_copy = send_one(dw_send, dw_recv, partner)
    with scope("s_gatherz"):
        arrive(gather_near)
        forward((0, *NEAR))
        arrive(gather_far)
        forward(FAR)
    with scope("s_gp"):
        arrive(dw_copy)
        dw_hat = dw_buf[c] + dw_recv[...].astype(F32)
        proto_unit, proto_inverse = unit_along(proto_ref[...], 0)
        gp_ref[...] = (
            (total_cols / math.sqrt(total_rows))
            * proto_inverse
            * (dw_hat - proto_unit * jnp.sum(proto_unit * dw_hat, axis=0, keepdims=True))
        )
    with scope("s_lossz"):
        lse = jnp.log(stud_total)
        part = lse[:, 0:128]
        for lane in range(128, rows, 128):
            part = part + lse[:, lane : lane + 128]
        loss_x[c] = part - finish(z_loss, loss_z)
        loss_copy = send_one(loss_x.at[c], loss_x.at[c], partner)
    def sent(some):
        for g in some:
            copy_of(g, groups[g], groups[g], partner).wait_send()

    with scope("s_sent"):
        early = [g for g in range(len(groups)) if g not in (gather_y, loss_copy)]
        sent(early)
    with scope("s_gathery"):
        arrive(gather_y)
    with scope("s_dz"):
        for i in range(NY):
            for q in range(NZ):
                r = 16 * (q // 2)
                s = half_own * (q % 2)
                base = i * piece + r if r < piece else half_k + i * piece + r - piece
                dzt[base : base + 16, s : s + half_own] = ygather[i, q].astype(F32)
        dz = jnp.transpose(dzt[...])
        stud_unit, stud_inverse = unit_along(stud_ref[...], 1)
        gs_ref[...] = stud_inverse * (
            dz - stud_unit * jnp.sum(stud_unit * dz, axis=1, keepdims=True)
        )
    with scope("s_end"):
        arrive(loss_copy)
        loss_ref[...] = jnp.broadcast_to(
            jnp.sum(loss_x[0] + loss_x[1], axis=1, keepdims=True) / total_rows, loss_ref.shape
        )
        assert len(groups) == GROUPS, len(groups)
        sent((gather_y, loss_copy))


def store_kernel(*refs):
    results, outs, sem = refs[:3], refs[3:6], refs[6]
    for i, (result, out) in enumerate(zip(results, outs)):
        pltpu.make_async_copy(result, out, sem.at[i]).start()
    for i, (result, out) in enumerate(zip(results, outs)):
        pltpu.make_async_copy(result, out, sem.at[i]).wait()


def solution(mesh):
    def shards(teacher_emb, student_emb, prototypes):
        own, k_dim = teacher_emb.shape
        cols = prototypes.shape[1]
        rows, both = NX * own, 2 * cols
        total_rows = own * mesh.shape["dp"]
        total_cols = cols * mesh.shape["dp"] * mesh.shape["proto"]
        vmem = pltpu.VMEM
        piece = k_dim // 8
        scratch = [
            vmem((own, k_dim), BF16),
            vmem((own, k_dim), BF16),
            vmem((k_dim, cols), BF16),
            vmem((NX, 4, k_dim, own // 4), BF16),
            vmem((NX, 4, k_dim, own // 4), BF16),
            vmem((NC, k_dim, cols), BF16),
            vmem((NC, cols, k_dim), BF16),
            vmem((k_dim + 16, both), BF16),
            vmem((NX, both, own), BF16),
            vmem((NX, own, both), BF16),
            vmem((NX, both, own), BF16),
            vmem((both, 128), F32),
            vmem((ITERS, NC, 1, both), F32),
            vmem((ITERS + 1, NX * NY, 1, rows), F32),
            vmem((ITERS + 1, NZ, 1, rows), F32),
            vmem((NX * NY, 1, 128), F32),
            vmem((NZ, 1, 128), F32),
            vmem((2, NX, 2, k_dim // 4, own), BF16),
            vmem((2, NY, 2, NX, piece // 2, own), BF16),
            vmem((2, 2, k_dim // 4, own), BF16),
            vmem((2, 2, NX, piece // 2, own), BF16),
            vmem((2, 2, k_dim // 4, own), BF16),
            vmem((2, 2, NX, piece // 2, own), BF16),
            vmem((2, 2, 2, k_dim // 4, own), BF16),
            vmem((2, 2, 2, NX, piece // 2, own), BF16),
            vmem((2, NY, piece, own), BF16),
            vmem((2, NX, piece, own), BF16),
            vmem((2, NY, piece, own), BF16),
            vmem((2, NX, piece, own), BF16),
            vmem((2, NZ, 16, own // 2), BF16),
            vmem((2, NZ, 16, own // 2), BF16),
            vmem((NY, NZ, 16, own // 2), BF16),
            vmem((NX, 1, own), F32),
            vmem((2, 2 * NX, 1, own // 2), F32),
            vmem((2, k_dim, cols), F32),
            vmem((k_dim, cols), BF16),
            vmem((k_dim, cols), BF16),
            vmem((2, 1, 128), F32),
            vmem((k_dim, own), F32),
            pltpu.SemaphoreType.DMA((GROUPS,)),
            pltpu.SemaphoreType.DMA((GROUPS,)),
            pltpu.SemaphoreType.DMA((3,)),
        ]
        anywhere = pl.BlockSpec(memory_space=pl.ANY)
        in_vmem = pl.BlockSpec(memory_space=vmem)
        shapes = ((1, 128), (own, k_dim), (k_dim, cols))
        results = pl.pallas_call(
            functools.partial(kernel, float(total_rows), float(total_cols)),
            out_shape=tuple(vmem(shape, F32) for shape in shapes),
            in_specs=[anywhere] * 3,
            out_specs=[in_vmem] * 3,
            scratch_shapes=scratch,
            compiler_params=pltpu.CompilerParams(
                collective_id=0, has_side_effects=True, vmem_limit_bytes=60 << 20
            ),
            name="prototype_head",
        )(teacher_emb, student_emb, prototypes)
        loss, grad_student, grad_prototypes = pl.pallas_call(
            store_kernel,
            out_shape=tuple(jax.ShapeDtypeStruct(shape, F32) for shape in shapes),
            in_specs=[in_vmem] * 3,
            out_specs=[anywhere] * 3,
            scratch_shapes=[pltpu.SemaphoreType.DMA((3,))],
            name="store_results",
        )(*(pltpu.with_memory_space_constraint(result, vmem) for result in results))
        return loss[0, 0], grad_student, grad_prototypes

    in_specs = (P("dp", None), P("dp", None), P(None, ("dp", "proto")))
    out_specs = (P(), P("dp", None), P(None, ("dp", "proto")))
    return jax.shard_map(shards, mesh=mesh, in_specs=in_specs, out_specs=out_specs, check_vma=False)
```

```python
import functools
import math

import jax
import jax.numpy as jnp
from jax import lax
from jax.experimental import pallas as pl
from jax.experimental.pallas import tpu as pltpu
from jax.sharding import PartitionSpec as P

ITERS = 3
TEACHER_TEMP = 0.04
STUDENT_TEMP = 0.1
NORM_EPS = 1e-06
LOG2E = 1.4426950408889634
NX, NC, NY, NZ = 4, 2, 4, 8
GROUPS = 50

MESH = pl.DeviceIdType.MESH
scope = jax.named_scope
F32, BF16 = jnp.float32, jnp.bfloat16
NT = (((1,), (1,)), ((), ()))


def unit_along(values, axis):
    floats = values.astype(F32)
    inverse = lax.rsqrt(jnp.sum(floats * floats, axis=axis, keepdims=True) + NORM_EPS)
    return floats * inverse, inverse


def split_rows(vec):
    n = vec.shape[1]
    high = vec.astype(BF16).astype(F32)
    low = vec - high
    row = lax.broadcasted_iota(jnp.int32, (16, n), 0)
    both = jnp.where(row == 0, high, jnp.where(row == 1, low, 0.0))
    return both.astype(BF16)


def kernel(
    total_rows,
    total_cols,
    teach_hbm,
    stud_hbm,
    proto_hbm,
    loss_ref,
    gs_ref,
    gp_ref,
    stud_ref,
    proto_ref,
    teach_raw,
    stud_all,
    proto_all,
    protot_all,
    left,
    exp_t,
    exp_n,
    exp_s,
    acc,
    colx,
    xy_vec,
    z_vec,
    xy_loss,
    z_loss,
    send_a,
    send_b,
    far_a,
    far_b,
    sum_a,
    sum_b,
    recv_a,
    recv_b,
    send_a2,
    send_b2,
    recv_a2,
    recv_b2,
    zsend,
    zrecv,
    ygather,
    cross,
    fac_mix,
    dw_buf,
    dw_send,
    dw_recv,
    loss_x,
    dzt,
    ssem,
    rsem,
    lsem,
):
    d = lax.axis_index("dp")
    p = lax.axis_index("proto")
    x, c = d // NC, lax.rem(d, NC)
    z, y = p // NY, lax.rem(p, NY)
    own = stud_ref.shape[0]
    k_dim, cols = proto_ref.shape
    rows = NX * own
    both_cols = 2 * cols
    half_own = own // 2

    def at_x(k):
        return lax.rem(x + k, NX)

    def at_y(k):
        return lax.rem(y + k, NY)

    def at_z(k):
        return lax.rem(z + k, NZ)

    def dev(xx, cc, yy, zz):
        return (xx * NC + cc, zz * NY + yy)

    def x_dev(xx):
        return dev(xx, c, y, z)

    def y_dev(yy):
        return dev(x, c, yy, z)

    def z_dev(zz):
        return dev(x, c, y, zz)

    partner = dev(x, 1 - c, y, z)
    xy_peers = [dev(at_x(k // 4), c, at_y(k % 4), z) for k in range(1, 16)]
    z_peers = [z_dev(at_z(k)) for k in range(1, 8)]
    everyone = [partner] + xy_peers + z_peers
    AROUND = (2, 1, 3)

    barrier = pltpu.get_barrier_semaphore()
    for peer in everyone:
        pl.semaphore_signal(barrier, inc=1, device_id=peer, device_id_type=MESH)

    groups = []

    def group(span):
        groups.append(span)
        return len(groups) - 1

    def copy_of(g, src, dst, peer):
        return pltpu.make_async_remote_copy(
            src_ref=src,
            dst_ref=dst,
            send_sem=ssem.at[g],
            recv_sem=rsem.at[g],
            device_id=peer,
            device_id_type=MESH,
        )

    def send(g, src, dst, peer):
        copy_of(g, src, dst, peer).start()

    def send_one(src, dst, peer):
        g = group(src)
        send(g, src, dst, peer)
        return g

    def arrive(g):
        copy_of(g, groups[g], groups[g], partner).wait_recv()

    def local(src, dst, sem):
        copy = pltpu.make_async_copy(src, dst, lsem.at[sem])
        copy.start()
        return copy

    quarter = own // 4

    def put_own(blocks, hat):
        hat_t = jnp.transpose(hat).astype(BF16)
        for q in range(4):
            blocks[x, q] = hat_t[:, q * quarter : (q + 1) * quarter]

    def start_gather(source, blocks):
        far = send_one(source.at[y], blocks.at[x, y], x_dev(at_x(2)))
        mine = 2 + lax.rem(z, 2)
        first = {
            k: send_one(source.at[mine], blocks.at[x, mine], x_dev(at_x(k))) for k in (1, 3)
        }
        rest = []
        for q in (0, 1):
            rest.append(group(blocks.at[0, pl.ds(0, 2)]))
            for k in (1, 3):
                send(rest[q], source.at[q], blocks.at[x, q], x_dev(at_x(k)))
        return far, first, *rest

    def relay_near(blocks, copies):
        mine = 2 + lax.rem(z, 2)
        g = group(blocks.at[0, pl.ds(0, 2)])
        for k, to in ((1, 1), (3, NZ - 1)):
            source = at_x(NX - k)
            arrive(copies[1][k])
            send(g, blocks.at[source, mine], blocks.at[source, mine], z_dev(at_z(to)))
        return g

    def relay_far(blocks, copies):
        source = at_x(2)
        arrive(copies[0])
        g = group(blocks.at[0, pl.ds(0, 3)])
        for k in AROUND:
            send(g, blocks.at[source, y], blocks.at[source, y], y_dev(at_y(k)))
        return g

    def block_of(blocks, j):
        return jnp.concatenate([blocks[j, q] for q in range(4)], axis=1)

    def pair_of(blocks, j, pair):
        return jnp.concatenate([blocks[j, q] for q in pair], axis=1)

    teach_load = local(teach_hbm, teach_raw.at[x], 0)
    proto_load = local(proto_hbm, proto_ref, 1)
    stud_load = local(stud_hbm, stud_ref, 2)
    with scope("s_barrier"):
        pl.semaphore_wait(barrier, len(everyone))
    with scope("s_norm"):
        teach_copies = start_gather(teach_hbm, teach_raw)
        proto_load.wait()
        proto_unit = unit_along(proto_ref[...], 0)[0]
        protot_all[c] = jnp.transpose(proto_unit).astype(BF16)
        protot_copy = send_one(protot_all.at[c], protot_all.at[c], partner)
        proto_all[c] = proto_unit.astype(BF16)
        proto_copy = send_one(proto_all.at[c], proto_all.at[c], partner)
        stud_load.wait()
        put_own(stud_all, unit_along(stud_ref[...], 1)[0])
        stud_copies = start_gather(stud_all.at[x], stud_all)

    def lanes_of(q):
        start = q * quarter
        return pl.ds(start if isinstance(q, int) else pl.multiple_of(start, quarter), quarter)

    def teacher_part(block, pair, half=None):
        if half is None:
            protos_t, rows_out = protot_all[...].reshape(both_cols, k_dim), slice(None)
        else:
            protos_t = protot_all[half]
            rows_out = pl.ds(pl.multiple_of(half * cols, cols), cols)
        hats = [unit_along(teach_raw[block, q], 1)[0].astype(BF16) for q in pair]
        prod = lax.dot_general(
            protos_t, jnp.concatenate(hats, axis=0), NT, preferred_element_type=F32
        )
        e = jnp.exp2(prod * (LOG2E / TEACHER_TEMP))
        low = e.astype(BF16)
        for i, q in enumerate(pair):
            exp_t[block, rows_out, lanes_of(q)] = low[:, i * quarter : (i + 1) * quarter]
        part = e[:, 0:128]
        for lane in range(128, half_own, 128):
            part = part + e[:, lane : lane + 128]
        acc[rows_out, :] += part

    def student_block(block):
        for pair in ((0, 1), (2, 3)):
            prod = jnp.dot(
                protot_all[...].reshape(both_cols, k_dim),
                pair_of(stud_all, block, pair),
                preferred_element_type=F32,
            )
            low = jnp.exp2(prod * (LOG2E / STUDENT_TEMP)).astype(BF16)
            exp_s[block, :, pair[0] * quarter : (pair[1] + 1) * quarter] = low

    with scope("s_T_own"):
        acc[...] = jnp.zeros_like(acc)
        teach_load.wait()
        teacher_part(x, (0, 1), c)
        teacher_part(x, (2, 3), c)
        arrive(protot_copy)
        teacher_part(x, (0, 1), 1 - c)
        teacher_part(x, (2, 3), 1 - c)
    with scope("s_relay"):
        teach_near = relay_near(teach_raw, teach_copies)
        teach_far = relay_far(teach_raw, teach_copies)
    with scope("s_direct"):
        arrive(teach_copies[2])
    mine = 2 + lax.rem(z, 2)
    with scope("s_T_early"):
        for k in (1, 3):
            teacher_part(at_x(k), (0, mine))
    with scope("s_relay_wait"):
        arrive(teach_copies[3])
        arrive(teach_near)
    with scope("s_T_late"):
        for k in (1, 3):
            teacher_part(at_x(k), (1, 5 - mine))
    with scope("s_far_wait"):
        arrive(teach_far)
    with scope("s_T_far"):
        teacher_part(at_x(2), (0, 1))
        teacher_part(at_x(2), (2, 3))

    def start_column_scale(step, sums):
        colx[step, c] = sums
        return send_one(colx.at[step, c], colx.at[step, c], partner)

    def finish_column_scale(step, g):
        arrive(g)
        return 1.0 / (total_cols * (colx[step, 0] + colx[step, 1]))

    def column_scale(step, sums):
        return finish_column_scale(step, start_column_scale(step, sums))

    def first_column_sums():
        parts = []
        for b in range(both_cols // 128):
            t = jnp.transpose(acc[b * 128 : (b + 1) * 128, :])
            parts.append(jnp.sum(t, axis=0, keepdims=True))
        return jnp.concatenate(parts, axis=1)

    def column_sums(row_scale):
        both = split_rows(row_scale)
        total = None
        for j in range(NX):
            part = jnp.dot(
                both[:, j * own : (j + 1) * own], exp_n[j], preferred_element_type=F32
            )
            total = part if total is None else total + part
        return total[0:1] + total[1:2]

    def row_sums(col_scale):
        both = split_rows(col_scale)
        parts = []
        for j in range(NX):
            part = jnp.dot(both, exp_t[j], preferred_element_type=F32)
            parts.append(part[0:1] + part[1:2])
        return jnp.concatenate(parts, axis=1)

    xy_me = x * NY + y

    def send_xy(buf):
        g = group(buf.at[pl.ds(0, 15)])
        for peer in xy_peers:
            send(g, buf.at[xy_me], buf.at[xy_me], peer)
        return g

    def start_xy(buf, vec):
        buf[xy_me] = vec
        return send_xy(buf)

    def send_z(buf):
        g = group(buf.at[pl.ds(0, 7)])
        for peer in z_peers:
            send(g, buf.at[z], buf.at[z], peer)
        return g

    def start_z(buf, vec):
        buf[z] = vec
        return send_z(buf)

    def finish(buf, g):
        arrive(g)
        total = buf[0]
        for i in range(1, buf.shape[0]):
            total = total + buf[i]
        return total

    half_k, piece = k_dim // 2, k_dim // 8

    def put_block(which, j, value):
        low = value.astype(BF16)
        for h in range(2):
            send_a[which, j, h] = low[h * half_k // 2 : (h + 1) * half_k // 2]
        for q in range(NY):
            for h in range(2):
                r = half_k + q * piece + h * piece // 2
                send_b[which, q, h, j] = low[r : r + piece // 2]

    B_STEPS = ((2, 1), (3, 0))

    def first_groups(which):
        half = far_b.at[which, 0]
        return [group(ref) for ref in (far_a.at[which], recv_a.at[which], half, recv_b.at[which], half)]

    def send_block(which, first, k):
        j = at_x(k)
        if k == 2:
            send(first[0], send_a.at[which, j, 0], far_a.at[which, 0], x_dev(at_x(1)))
            send(first[0], send_a.at[which, j, 1], far_a.at[which, 1], x_dev(at_x(3)))
        if k == 1:
            send(first[1], send_a.at[which, j, 1], recv_a.at[which, 0, 1], x_dev(j))
        if k == 3:
            send(first[1], send_a.at[which, j, 0], recv_a.at[which, 1, 0], x_dev(j))
        up, down, far = at_y(1), at_y(3), at_y(2)
        g = first[2] if k in B_STEPS[0] else first[4]
        send(g, send_b.at[which, far, 0, j], far_b.at[which, 0, j], y_dev(up))
        send(g, send_b.at[which, far, 1, j], far_b.at[which, 1, j], y_dev(down))
        send(first[3], send_b.at[which, up, 1, j], recv_b.at[which, 0, 1, j], y_dev(up))
        send(first[3], send_b.at[which, down, 0, j], recv_b.at[which, 1, 0, j], y_dev(down))

    def pass_on_a(which, first):
        arrive(first[0])
        for h, k in ((0, 1), (1, 3)):
            both = send_a[which, at_x(k), h].astype(F32) + far_a[which, h].astype(F32)
            sum_a[which, h] = both.astype(BF16)
            send(first[1], sum_a.at[which, h], recv_a.at[which, h, h], x_dev(at_x(k)))

    def pass_on_b(which, first, step):
        arrive(first[4 if step else 2])
        for h, k in ((0, 1), (1, 3)):
            for i in B_STEPS[step]:
                j = at_x(i)
                both = send_b[which, at_y(k), h, j].astype(F32) + far_b[which, h, j].astype(F32)
                sum_b[which, h, j] = both.astype(BF16)
                send(first[3], sum_b.at[which, h, j], recv_b.at[which, h, h, j], y_dev(at_y(k)))

    def start_second(which, first):
        arrive(first[1])
        total = send_a[which, x].astype(F32)
        for i in range(2):
            total = total + recv_a[which, i].astype(F32)
        low = total.astype(BF16).reshape(half_k, own)
        for q in range(NY):
            send_a2[which, q] = low[q * piece : (q + 1) * piece]
        a2 = group(recv_a2.at[which, pl.ds(0, 3)])
        for k in AROUND:
            send(a2, send_a2.at[which, at_y(k)], recv_a2.at[which, y], y_dev(at_y(k)))
        arrive(first[3])
        for j in range(NX):
            total = send_b[which, y, :, j].astype(F32)
            for i in range(2):
                total = total + recv_b[which, i, :, j].astype(F32)
            send_b2[which, j] = total.astype(BF16).reshape(piece, own)
        b2 = group(recv_b2.at[which, pl.ds(0, 3)])
        for k in AROUND:
            send(b2, send_b2.at[which, at_x(k)], recv_b2.at[which, x], x_dev(at_x(k)))
        return a2, b2

    def start_third(which, second):
        a2, b2 = second
        recv_a2[which, y] = send_a2[which, y]
        recv_b2[which, x] = send_b2[which, x]
        arrive(a2)
        arrive(b2)
        low = recv_a2[which, 0].astype(F32)
        high = recv_b2[which, 0].astype(F32)
        for i in range(1, 4):
            low = low + recv_a2[which, i].astype(F32)
            high = high + recv_b2[which, i].astype(F32)
        low, high = low.astype(BF16), high.astype(BF16)
        for q in range(NZ):
            r = 16 * (q // 2)
            s = half_own * (q % 2)
            part = low[r : r + 16] if r < piece else high[r - piece : r - piece + 16]
            zsend[which, q] = part[:, s : s + half_own]
        third = group(zrecv.at[which, pl.ds(0, 7)])
        for k in range(1, NZ):
            send(third, zsend.at[which, at_z(k)], zrecv.at[which, z], z_dev(at_z(k)))
        return third

    def finish_third(which, third):
        zrecv[which, z] = zsend[which, z]
        arrive(third)
        total = zrecv[which, 0].astype(F32)
        for i in range(1, NZ):
            total = total + zrecv[which, i].astype(F32)
        return total

    with scope("s_col1"):
        col_copy = start_column_scale(0, first_column_sums())
        stud_near = relay_near(stud_all, stud_copies)
        stud_far = relay_far(stud_all, stud_copies)
        scale = finish_column_scale(0, col_copy)
    with scope("s_row1"):
        xy_copies = start_xy(xy_vec.at[0], row_sums(scale))
    with scope("s_S_own"):
        student_block(x)
    with scope("s_transpose"):
        for j in range(NX):
            for b in range(both_cols // 128):
                for a in range(own // 128):
                    exp_n[j, a * 128 : (a + 1) * 128, b * 128 : (b + 1) * 128] = jnp.transpose(
                        exp_t[j, b * 128 : (b + 1) * 128, a * 128 : (a + 1) * 128]
                    )
    with scope("s_stud_wait"):
        arrive(stud_copies[2])
        arrive(stud_copies[3])
        arrive(stud_near)
        student_block(at_x(1))
    with scope("s_xy1"):
        z_copies = start_z(z_vec.at[0], finish(xy_vec.at[0], xy_copies))
    with scope("s_S_near"):
        student_block(at_x(3))
    with scope("s_S_far"):
        arrive(stud_far)
        student_block(at_x(2))
    with scope("s_P1"):
        arrive(proto_copy)
        left[0:k_dim, 0:cols] = proto_all[0]
        left[0:k_dim, cols:] = proto_all[1]
        left[k_dim:, :] = jnp.ones((16, both_cols), BF16)
        stud_sums = []
        for j in range(NX):
            value = jnp.dot(left[...], exp_s[j], preferred_element_type=F32)
            put_block(0, j, value[0:k_dim])
            stud_sums.append(value[k_dim : k_dim + 1])
        stud_xy = start_xy(xy_vec.at[3], jnp.concatenate(stud_sums, axis=1))
    with scope("s_z1"):
        row_scale = 1.0 / (total_rows * finish(z_vec.at[0], z_copies))

    with scope("s_col2"):
        sums = column_sums(row_scale)
    with scope("s_colx2"):
        scale = column_scale(1, sums)
    with scope("s_row2"):
        xy_copies = start_xy(xy_vec.at[1], row_sums(scale))
        first1 = first_groups(0)
        for k in (2, 1, 3, 0):
            send_block(0, first1, k)
    with scope("s_studxy"):
        stud_z = start_z(z_vec.at[3], finish(xy_vec.at[3], stud_xy))
    with scope("s_xy2"):
        z_copies = start_z(z_vec.at[1], finish(xy_vec.at[1], xy_copies))
    with scope("s_pass1"):
        pass_on_a(0, first1)
        pass_on_b(0, first1, 0)
        pass_on_b(0, first1, 1)
    with scope("s_z2"):
        row_scale = 1.0 / (total_rows * finish(z_vec.at[1], z_copies))

    with scope("s_col3"):
        sums = column_sums(row_scale)
    with scope("s_colx3"):
        col_copy = start_column_scale(2, sums)
        second1 = start_second(0, first1)
        scale = finish_column_scale(2, col_copy)
    with scope("s_P2"):
        for h in range(NC):
            left[0:k_dim, h * cols : (h + 1) * cols] = (
                proto_all[h].astype(F32) * scale[:, h * cols : (h + 1) * cols]
            ).astype(BF16)
        left[k_dim:, :] = split_rows(scale)
        first2 = first_groups(1)
        for k in (2, 1, 3, 0):
            j = at_x(k)
            value = jnp.dot(left[...], exp_t[j], preferred_element_type=F32)
            put_block(1, j, value[0:k_dim])
            send_block(1, first2, k)
            z_vec[2, z, :, pl.ds(pl.multiple_of(j * own, own), own)] = (
                value[k_dim : k_dim + 1] + value[k_dim + 1 : k_dim + 2]
            )
            cross[j] = jnp.sum(
                value[0:k_dim] * block_of(stud_all, j).astype(F32), axis=0, keepdims=True
            )
        z_copies = send_z(z_vec.at[2])
    with scope("s_pass2a"):
        pass_on_b(1, first2, 0)
        pass_on_a(1, first2)
    with scope("s_third1"):
        third1 = start_third(0, second1)
    with scope("s_pass2b"):
        pass_on_b(1, first2, 1)

    with scope("s_second2"):
        second2 = start_second(1, first2)
    with scope("s_z3"):
        xy_copies = start_xy(xy_vec.at[2], finish(z_vec.at[2], z_copies))

    with scope("s_dwS"):
        stud_total = finish(z_vec.at[3], stud_z)
        stud_factor = (1.0 / STUDENT_TEMP) / stud_total
        for h in range(NC):
            total = None
            for j in range(NX):
                weights = (
                    block_of(stud_all, j).astype(F32) * stud_factor[:, j * own : (j + 1) * own]
                ).astype(BF16)
                part = lax.dot_general(
                    weights,
                    exp_s[j, h * cols : (h + 1) * cols, :],
                    NT,
                    preferred_element_type=F32,
                )
                total = part if total is None else total + part
            dw_buf[h] = total
    with scope("s_third2"):
        third2 = start_third(1, second2)
    with scope("s_xy3"):
        row_scale = 1.0 / (total_rows * finish(xy_vec.at[2], xy_copies))
        teach_factor = (total_rows / STUDENT_TEMP) * row_scale

    with scope("s_loss"):
        part = None
        for j in range(NX):
            term = teach_factor[:, j * own : (j + 1) * own] * cross[j]
            for lane in range(0, own, 128):
                t = term[:, lane : lane + 128]
                part = t if part is None else part + t
        loss_xy = start_xy(xy_loss, part)

    with scope("s_mix"):
        part1 = finish_third(0, third1)
        part2 = finish_third(1, third2)
        for i in range(2 * NX):
            s = i * half_own
            fac_mix[0, i] = stud_factor[:, s : s + half_own]
            fac_mix[1, i] = teach_factor[:, s : s + half_own]
        mine = x * 2 + lax.rem(z, 2)
        ygather[y, z] = (fac_mix[0, mine] * part1 - fac_mix[1, mine] * part2).astype(BF16)
        NEAR, FAR = (1, 7, 2, 6), (3, 5, 4)
        gather_near = group(ygather.at[0, pl.ds(0, len(NEAR))])
        gather_far = group(ygather.at[0, pl.ds(0, len(FAR))])
        for g, steps in ((gather_far, FAR), (gather_near, NEAR)):
            for k in steps:
                send(g, ygather.at[y, z], ygather.at[y, z], z_dev(at_z(k)))
        gather_y = group(ygather.at[pl.ds(0, 3)])

        def forward(steps):
            for k in steps:
                sz = at_z(k)
                for h in AROUND:
                    send(gather_y, ygather.at[y, sz], ygather.at[y, sz], y_dev(at_y(h)))

    def teacher_half(h):
        total = None
        for j in range(NX):
            weights = (
                block_of(stud_all, j).astype(F32) * teach_factor[:, j * own : (j + 1) * own]
            ).astype(BF16)
            part = lax.dot_general(
                weights,
                exp_t[j, h * cols : (h + 1) * cols, :],
                NT,
                preferred_element_type=F32,
            )
            total = part if total is None else total + part
        dw_buf[h] = dw_buf[h] - total * scale[:, h * cols : (h + 1) * cols]

    with scope("s_dwT"):
        teacher_half(0)
    with scope("s_lossxy"):
        loss_z = start_z(z_loss, finish(xy_loss, loss_xy))
    with scope("s_dwT"):
        teacher_half(1)
        dw_send[...] = dw_buf[1 - c].astype(BF16)
        dw_copy = send_one(dw_send, dw_recv, partner)
    with scope("s_gatherz"):
        arrive(gather_near)
        forward((0, *NEAR))
        arrive(gather_far)
        forward(FAR)
    with scope("s_gp"):
        arrive(dw_copy)
        dw_hat = dw_buf[c] + dw_recv[...].astype(F32)
        proto_unit, proto_inverse = unit_along(proto_ref[...], 0)
        gp_ref[...] = (
            (total_cols / math.sqrt(total_rows))
            * proto_inverse
            * (dw_hat - proto_unit * jnp.sum(proto_unit * dw_hat, axis=0, keepdims=True))
        )
    with scope("s_lossz"):
        lse = jnp.log(stud_total)
        part = lse[:, 0:128]
        for lane in range(128, rows, 128):
            part = part + lse[:, lane : lane + 128]
        loss_x[c] = part - finish(z_loss, loss_z)
        loss_copy = send_one(loss_x.at[c], loss_x.at[c], partner)
    def sent(some):
        for g in some:
            copy_of(g, groups[g], groups[g], partner).wait_send()

    with scope("s_sent"):
        early = [g for g in range(len(groups)) if g not in (gather_y, loss_copy)]
        sent(early)
    with scope("s_gathery"):
        arrive(gather_y)
    with scope("s_dz"):
        for i in range(NY):
            for q in range(NZ):
                r = 16 * (q // 2)
                s = half_own * (q % 2)
                base = i * piece + r if r < piece else half_k + i * piece + r - piece
                dzt[base : base + 16, s : s + half_own] = ygather[i, q].astype(F32)
        dz = jnp.transpose(dzt[...])
        stud_unit, stud_inverse = unit_along(stud_ref[...], 1)
        gs_ref[...] = stud_inverse * (
            dz - stud_unit * jnp.sum(stud_unit * dz, axis=1, keepdims=True)
        )
    with scope("s_end"):
        arrive(loss_copy)
        loss_ref[...] = jnp.broadcast_to(
            jnp.sum(loss_x[0] + loss_x[1], axis=1, keepdims=True) / total_rows, loss_ref.shape
        )
        assert len(groups) == GROUPS, len(groups)
        sent((gather_y, loss_copy))


def store_kernel(*refs):
    results, outs, sem = refs[:3], refs[3:6], refs[6]
    for i, (result, out) in enumerate(zip(results, outs)):
        pltpu.make_async_copy(result, out, sem.at[i]).start()
    for i, (result, out) in enumerate(zip(results, outs)):
        pltpu.make_async_copy(result, out, sem.at[i]).wait()


def solution(mesh):
    def shards(teacher_emb, student_emb, prototypes):
        own, k_dim = teacher_emb.shape
        cols = prototypes.shape[1]
        rows, both = NX * own, 2 * cols
        total_rows = own * mesh.shape["dp"]
        total_cols = cols * mesh.shape["dp"] * mesh.shape["proto"]
        vmem = pltpu.VMEM
        piece = k_dim // 8
        scratch = [
            vmem((own, k_dim), BF16),
            vmem((k_dim, cols), BF16),
            vmem((NX, 4, own // 4, k_dim), BF16),
            vmem((NX, 4, k_dim, own // 4), BF16),
            vmem((NC, k_dim, cols), BF16),
            vmem((NC, cols, k_dim), BF16),
            vmem((k_dim + 16, both), BF16),
            vmem((NX, both, own), BF16),
            vmem((NX, own, both), BF16),
            vmem((NX, both, own), BF16),
            vmem((both, 128), F32),
            vmem((ITERS, NC, 1, both), F32),
            vmem((ITERS + 1, NX * NY, 1, rows), F32),
            vmem((ITERS + 1, NZ, 1, rows), F32),
            vmem((NX * NY, 1, 128), F32),
            vmem((NZ, 1, 128), F32),
            vmem((2, NX, 2, k_dim // 4, own), BF16),
            vmem((2, NY, 2, NX, piece // 2, own), BF16),
            vmem((2, 2, k_dim // 4, own), BF16),
            vmem((2, 2, NX, piece // 2, own), BF16),
            vmem((2, 2, k_dim // 4, own), BF16),
            vmem((2, 2, NX, piece // 2, own), BF16),
            vmem((2, 2, 2, k_dim // 4, own), BF16),
            vmem((2, 2, 2, NX, piece // 2, own), BF16),
            vmem((2, NY, piece, own), BF16),
            vmem((2, NX, piece, own), BF16),
            vmem((2, NY, piece, own), BF16),
            vmem((2, NX, piece, own), BF16),
            vmem((2, NZ, 16, own // 2), BF16),
            vmem((2, NZ, 16, own // 2), BF16),
            vmem((NY, NZ, 16, own // 2), BF16),
            vmem((NX, 1, own), F32),
            vmem((2, 2 * NX, 1, own // 2), F32),
            vmem((2, k_dim, cols), F32),
            vmem((k_dim, cols), BF16),
            vmem((k_dim, cols), BF16),
            vmem((2, 1, 128), F32),
            vmem((k_dim, own), F32),
            pltpu.SemaphoreType.DMA((GROUPS,)),
            pltpu.SemaphoreType.DMA((GROUPS,)),
            pltpu.SemaphoreType.DMA((3,)),
        ]
        anywhere = pl.BlockSpec(memory_space=pl.ANY)
        in_vmem = pl.BlockSpec(memory_space=vmem)
        shapes = ((1, 128), (own, k_dim), (k_dim, cols))
        results = pl.pallas_call(
            functools.partial(kernel, float(total_rows), float(total_cols)),
            out_shape=tuple(vmem(shape, F32) for shape in shapes),
            in_specs=[anywhere] * 3,
            out_specs=[in_vmem] * 3,
            scratch_shapes=scratch,
            compiler_params=pltpu.CompilerParams(
                collective_id=0, has_side_effects=True, vmem_limit_bytes=60 << 20
            ),
            name="prototype_head",
        )(teacher_emb.reshape(4, own // 4, k_dim), student_emb, prototypes)
        loss, grad_student, grad_prototypes = pl.pallas_call(
            store_kernel,
            out_shape=tuple(jax.ShapeDtypeStruct(shape, F32) for shape in shapes),
            in_specs=[in_vmem] * 3,
            out_specs=[anywhere] * 3,
            scratch_shapes=[pltpu.SemaphoreType.DMA((3,))],
            name="store_results",
        )(*(pltpu.with_memory_space_constraint(result, vmem) for result in results))
        return loss[0, 0], grad_student, grad_prototypes

    in_specs = (P("dp", None), P("dp", None), P(None, ("dp", "proto")))
    out_specs = (P(), P("dp", None), P(None, ("dp", "proto")))
    return jax.shard_map(shards, mesh=mesh, in_specs=in_specs, out_specs=out_specs, check_vma=False)
```

```python
import functools
import math

import jax
import jax.numpy as jnp
from jax import lax
from jax.experimental import pallas as pl
from jax.experimental.pallas import tpu as pltpu
from jax.sharding import PartitionSpec as P

ITERS = 3
TEACHER_TEMP = 0.04
STUDENT_TEMP = 0.1
NORM_EPS = 1e-06
LOG2E = 1.4426950408889634
NX, NC, NY, NZ = 4, 2, 4, 8
GROUPS = 54

MESH = pl.DeviceIdType.MESH
scope = jax.named_scope
F32, BF16 = jnp.float32, jnp.bfloat16
NT = (((1,), (1,)), ((), ()))


def unit_along(values, axis):
    floats = values.astype(F32)
    inverse = lax.rsqrt(jnp.sum(floats * floats, axis=axis, keepdims=True) + NORM_EPS)
    return floats * inverse, inverse


def split_rows(vec):
    n = vec.shape[1]
    high = vec.astype(BF16).astype(F32)
    low = vec - high
    row = lax.broadcasted_iota(jnp.int32, (16, n), 0)
    both = jnp.where(row == 0, high, jnp.where(row == 1, low, 0.0))
    return both.astype(BF16)


def kernel(
    total_rows,
    total_cols,
    teach_hbm,
    stud_hbm,
    proto_hbm,
    loss_ref,
    gs_ref,
    gp_ref,
    stud_ref,
    proto_ref,
    teach_raw,
    stud_all,
    proto_all,
    protot_all,
    left,
    exp_t,
    exp_n,
    exp_s,
    acc,
    colx,
    xy_half,
    z_half,
    xy_vec,
    z_vec,
    xy_loss,
    z_loss,
    send_a,
    send_b,
    far_a,
    far_b,
    sum_a,
    sum_b,
    recv_a,
    recv_b,
    send_a2,
    send_b2,
    recv_a2,
    recv_b2,
    zsend,
    zrecv,
    ygather,
    cross,
    fac_mix,
    dw_buf,
    dw_send,
    dw_recv,
    loss_x,
    dzt,
    ssem,
    rsem,
    lsem,
):
    d = lax.axis_index("dp")
    p = lax.axis_index("proto")
    x, c = d // NC, lax.rem(d, NC)
    z, y = p // NY, lax.rem(p, NY)
    own = stud_ref.shape[0]
    k_dim, cols = proto_ref.shape
    rows = NX * own
    both_cols = 2 * cols
    half_own = own // 2

    def at_x(k):
        return lax.rem(x + k, NX)

    def at_y(k):
        return lax.rem(y + k, NY)

    def at_z(k):
        return lax.rem(z + k, NZ)

    def dev(xx, cc, yy, zz):
        return (xx * NC + cc, zz * NY + yy)

    def x_dev(xx):
        return dev(xx, c, y, z)

    def y_dev(yy):
        return dev(x, c, yy, z)

    def z_dev(zz):
        return dev(x, c, y, zz)

    partner = dev(x, 1 - c, y, z)
    xy_peers = [dev(at_x(k // 4), c, at_y(k % 4), z) for k in range(1, 16)]
    z_peers = [z_dev(at_z(k)) for k in range(1, 8)]
    everyone = [partner] + xy_peers + z_peers
    AROUND = (2, 1, 3)

    barrier = pltpu.get_barrier_semaphore()
    for peer in everyone:
        pl.semaphore_signal(barrier, inc=1, device_id=peer, device_id_type=MESH)

    groups = []

    def group(span):
        groups.append(span)
        return len(groups) - 1

    def copy_of(g, src, dst, peer):
        return pltpu.make_async_remote_copy(
            src_ref=src,
            dst_ref=dst,
            send_sem=ssem.at[g],
            recv_sem=rsem.at[g],
            device_id=peer,
            device_id_type=MESH,
        )

    def send(g, src, dst, peer):
        copy_of(g, src, dst, peer).start()

    def send_one(src, dst, peer):
        g = group(src)
        send(g, src, dst, peer)
        return g

    def arrive(g):
        copy_of(g, groups[g], groups[g], partner).wait_recv()

    def local(src, dst, sem):
        copy = pltpu.make_async_copy(src, dst, lsem.at[sem])
        copy.start()
        return copy

    quarter = own // 4

    def put_own(blocks, hat):
        hat_t = jnp.transpose(hat).astype(BF16)
        for q in range(4):
            blocks[x, q] = hat_t[:, q * quarter : (q + 1) * quarter]

    def start_gather(source, blocks):
        far = send_one(source.at[y], blocks.at[x, y], x_dev(at_x(2)))
        mine = 2 + lax.rem(z, 2)
        first = {
            k: send_one(source.at[mine], blocks.at[x, mine], x_dev(at_x(k))) for k in (1, 3)
        }
        rest = []
        for q in (0, 1):
            rest.append(group(blocks.at[0, pl.ds(0, 2)]))
            for k in (1, 3):
                send(rest[q], source.at[q], blocks.at[x, q], x_dev(at_x(k)))
        return far, first, *rest

    def relay_near(blocks, copies):
        mine = 2 + lax.rem(z, 2)
        g = group(blocks.at[0, pl.ds(0, 2)])
        for k, to in ((1, 1), (3, NZ - 1)):
            source = at_x(NX - k)
            arrive(copies[1][k])
            send(g, blocks.at[source, mine], blocks.at[source, mine], z_dev(at_z(to)))
        return g

    def relay_far(blocks, copies):
        source = at_x(2)
        arrive(copies[0])
        g = group(blocks.at[0, pl.ds(0, 3)])
        for k in AROUND:
            send(g, blocks.at[source, y], blocks.at[source, y], y_dev(at_y(k)))
        return g

    def block_of(blocks, j):
        return jnp.concatenate([blocks[j, q] for q in range(4)], axis=1)

    def pair_of(blocks, j, pair):
        return jnp.concatenate([blocks[j, q] for q in pair], axis=1)

    teach_load = local(teach_hbm, teach_raw.at[x], 0)
    proto_load = local(proto_hbm, proto_ref, 1)
    stud_load = local(stud_hbm, stud_ref, 2)
    with scope("s_barrier"):
        pl.semaphore_wait(barrier, len(everyone))
    with scope("s_norm"):
        teach_copies = start_gather(teach_hbm, teach_raw)
        proto_load.wait()
        proto_unit = unit_along(proto_ref[...], 0)[0]
        protot_all[c] = jnp.transpose(proto_unit).astype(BF16)
        protot_copy = send_one(protot_all.at[c], protot_all.at[c], partner)
        proto_all[c] = proto_unit.astype(BF16)
        proto_copy = send_one(proto_all.at[c], proto_all.at[c], partner)
        stud_load.wait()
        put_own(stud_all, unit_along(stud_ref[...], 1)[0])
        stud_copies = start_gather(stud_all.at[x], stud_all)

    def lanes_of(q):
        start = q * quarter
        return pl.ds(start if isinstance(q, int) else pl.multiple_of(start, quarter), quarter)

    def teacher_part(block, pair, half=None):
        if half is None:
            protos_t, rows_out = protot_all[...].reshape(both_cols, k_dim), slice(None)
        else:
            protos_t = protot_all[half]
            rows_out = pl.ds(pl.multiple_of(half * cols, cols), cols)
        hats = [unit_along(teach_raw[block, q], 1)[0].astype(BF16) for q in pair]
        prod = lax.dot_general(
            protos_t, jnp.concatenate(hats, axis=0), NT, preferred_element_type=F32
        )
        e = jnp.exp2(prod * (LOG2E / TEACHER_TEMP))
        low = e.astype(BF16)
        for i, q in enumerate(pair):
            exp_t[block, rows_out, lanes_of(q)] = low[:, i * quarter : (i + 1) * quarter]
        part = e[:, 0:128]
        for lane in range(128, half_own, 128):
            part = part + e[:, lane : lane + 128]
        acc[rows_out, :] += part

    def student_block(block):
        for pair in ((0, 1), (2, 3)):
            prod = jnp.dot(
                protot_all[...].reshape(both_cols, k_dim),
                pair_of(stud_all, block, pair),
                preferred_element_type=F32,
            )
            low = jnp.exp2(prod * (LOG2E / STUDENT_TEMP)).astype(BF16)
            exp_s[block, :, pair[0] * quarter : (pair[1] + 1) * quarter] = low

    with scope("s_T_own"):
        acc[...] = jnp.zeros_like(acc)
        teach_load.wait()
        teacher_part(x, (0, 1), c)
        teacher_part(x, (2, 3), c)
        arrive(protot_copy)
        teacher_part(x, (0, 1), 1 - c)
        teacher_part(x, (2, 3), 1 - c)
    with scope("s_relay"):
        teach_near = relay_near(teach_raw, teach_copies)
        teach_far = relay_far(teach_raw, teach_copies)
    with scope("s_direct"):
        arrive(teach_copies[2])
    mine = 2 + lax.rem(z, 2)
    with scope("s_T_early"):
        for k in (1, 3):
            teacher_part(at_x(k), (0, mine))
    with scope("s_relay_wait"):
        arrive(teach_copies[3])
        arrive(teach_near)
    with scope("s_T_late"):
        for k in (1, 3):
            teacher_part(at_x(k), (1, 5 - mine))
    with scope("s_far_wait"):
        arrive(teach_far)
    with scope("s_T_far"):
        teacher_part(at_x(2), (0, 1))
        teacher_part(at_x(2), (2, 3))

    def start_column_scale(step, sums):
        colx[step, c] = sums
        return send_one(colx.at[step, c], colx.at[step, c], partner)

    def finish_column_scale(step, g):
        arrive(g)
        return 1.0 / (total_cols * (colx[step, 0] + colx[step, 1]))

    def column_scale(step, sums):
        return finish_column_scale(step, start_column_scale(step, sums))

    def first_column_sums():
        parts = []
        for b in range(both_cols // 128):
            t = jnp.transpose(acc[b * 128 : (b + 1) * 128, :])
            parts.append(jnp.sum(t, axis=0, keepdims=True))
        return jnp.concatenate(parts, axis=1)

    HALVES = ((0, 1), (2, 3))

    def column_sums(step, z_copies):
        total = None
        for p, blocks in enumerate(HALVES):
            row_scale = 1.0 / (total_rows * finish(z_half.at[step, p], z_copies[p]))
            both = split_rows(row_scale)
            for i, j in enumerate(blocks):
                part = jnp.dot(
                    both[:, i * own : (i + 1) * own], exp_n[j], preferred_element_type=F32
                )
                total = part if total is None else total + part
        return total[0:1] + total[1:2]

    def start_rows(step, col_scale):
        both = split_rows(col_scale)
        copies = []
        for p, blocks in enumerate(HALVES):
            parts = []
            for j in blocks:
                part = jnp.dot(both, exp_t[j], preferred_element_type=F32)
                parts.append(part[0:1] + part[1:2])
            copies.append(start_xy(xy_half.at[step, p], jnp.concatenate(parts, axis=1)))
        return copies

    def rows_on_z(step, copies):
        return [
            start_z(z_half.at[step, p], finish(xy_half.at[step, p], copies[p])) for p in range(2)
        ]

    xy_me = x * NY + y

    def send_xy(buf):
        g = group(buf.at[pl.ds(0, 15)])
        for peer in xy_peers:
            send(g, buf.at[xy_me], buf.at[xy_me], peer)
        return g

    def start_xy(buf, vec):
        buf[xy_me] = vec
        return send_xy(buf)

    def send_z(buf):
        g = group(buf.at[pl.ds(0, 7)])
        for peer in z_peers:
            send(g, buf.at[z], buf.at[z], peer)
        return g

    def start_z(buf, vec):
        buf[z] = vec
        return send_z(buf)

    def finish(buf, g):
        arrive(g)
        total = buf[0]
        for i in range(1, buf.shape[0]):
            total = total + buf[i]
        return total

    half_k, piece = k_dim // 2, k_dim // 8

    def put_block(which, j, value):
        low = value.astype(BF16)
        for h in range(2):
            send_a[which, j, h] = low[h * half_k // 2 : (h + 1) * half_k // 2]
        for q in range(NY):
            for h in range(2):
                r = half_k + q * piece + h * piece // 2
                send_b[which, q, h, j] = low[r : r + piece // 2]

    B_STEPS = ((2, 1), (3, 0))

    def first_groups(which):
        half = far_b.at[which, 0]
        return [group(ref) for ref in (far_a.at[which], recv_a.at[which], half, recv_b.at[which], half)]

    def send_block(which, first, k):
        j = at_x(k)
        if k == 2:
            send(first[0], send_a.at[which, j, 0], far_a.at[which, 0], x_dev(at_x(1)))
            send(first[0], send_a.at[which, j, 1], far_a.at[which, 1], x_dev(at_x(3)))
        if k == 1:
            send(first[1], send_a.at[which, j, 1], recv_a.at[which, 0, 1], x_dev(j))
        if k == 3:
            send(first[1], send_a.at[which, j, 0], recv_a.at[which, 1, 0], x_dev(j))
        up, down, far = at_y(1), at_y(3), at_y(2)
        g = first[2] if k in B_STEPS[0] else first[4]
        send(g, send_b.at[which, far, 0, j], far_b.at[which, 0, j], y_dev(up))
        send(g, send_b.at[which, far, 1, j], far_b.at[which, 1, j], y_dev(down))
        send(first[3], send_b.at[which, up, 1, j], recv_b.at[which, 0, 1, j], y_dev(up))
        send(first[3], send_b.at[which, down, 0, j], recv_b.at[which, 1, 0, j], y_dev(down))

    def pass_on_a(which, first):
        arrive(first[0])
        for h, k in ((0, 1), (1, 3)):
            both = send_a[which, at_x(k), h].astype(F32) + far_a[which, h].astype(F32)
            sum_a[which, h] = both.astype(BF16)
            send(first[1], sum_a.at[which, h], recv_a.at[which, h, h], x_dev(at_x(k)))

    def pass_on_b(which, first, step):
        arrive(first[4 if step else 2])
        for h, k in ((0, 1), (1, 3)):
            for i in B_STEPS[step]:
                j = at_x(i)
                both = send_b[which, at_y(k), h, j].astype(F32) + far_b[which, h, j].astype(F32)
                sum_b[which, h, j] = both.astype(BF16)
                send(first[3], sum_b.at[which, h, j], recv_b.at[which, h, h, j], y_dev(at_y(k)))

    def start_second(which, first):
        arrive(first[1])
        total = send_a[which, x].astype(F32)
        for i in range(2):
            total = total + recv_a[which, i].astype(F32)
        low = total.astype(BF16).reshape(half_k, own)
        for q in range(NY):
            send_a2[which, q] = low[q * piece : (q + 1) * piece]
        a2 = group(recv_a2.at[which, pl.ds(0, 3)])
        for k in AROUND:
            send(a2, send_a2.at[which, at_y(k)], recv_a2.at[which, y], y_dev(at_y(k)))
        arrive(first[3])
        for j in range(NX):
            total = send_b[which, y, :, j].astype(F32)
            for i in range(2):
                total = total + recv_b[which, i, :, j].astype(F32)
            send_b2[which, j] = total.astype(BF16).reshape(piece, own)
        b2 = group(recv_b2.at[which, pl.ds(0, 3)])
        for k in AROUND:
            send(b2, send_b2.at[which, at_x(k)], recv_b2.at[which, x], x_dev(at_x(k)))
        return a2, b2

    def start_third(which, second):
        a2, b2 = second
        recv_a2[which, y] = send_a2[which, y]
        recv_b2[which, x] = send_b2[which, x]
        arrive(a2)
        arrive(b2)
        low = recv_a2[which, 0].astype(F32)
        high = recv_b2[which, 0].astype(F32)
        for i in range(1, 4):
            low = low + recv_a2[which, i].astype(F32)
            high = high + recv_b2[which, i].astype(F32)
        low, high = low.astype(BF16), high.astype(BF16)
        for q in range(NZ):
            r = 16 * (q // 2)
            s = half_own * (q % 2)
            part = low[r : r + 16] if r < piece else high[r - piece : r - piece + 16]
            zsend[which, q] = part[:, s : s + half_own]
        third = group(zrecv.at[which, pl.ds(0, 7)])
        for k in range(1, NZ):
            send(third, zsend.at[which, at_z(k)], zrecv.at[which, z], z_dev(at_z(k)))
        return third

    def finish_third(which, third):
        zrecv[which, z] = zsend[which, z]
        arrive(third)
        total = zrecv[which, 0].astype(F32)
        for i in range(1, NZ):
            total = total + zrecv[which, i].astype(F32)
        return total

    with scope("s_col1"):
        col_copy = start_column_scale(0, first_column_sums())
        stud_near = relay_near(stud_all, stud_copies)
        stud_far = relay_far(stud_all, stud_copies)
        scale = finish_column_scale(0, col_copy)
    with scope("s_row1"):
        xy_copies = start_rows(0, scale)
    with scope("s_S_own"):
        student_block(x)
    with scope("s_transpose"):
        for j in range(NX):
            for b in range(both_cols // 128):
                for a in range(own // 128):
                    exp_n[j, a * 128 : (a + 1) * 128, b * 128 : (b + 1) * 128] = jnp.transpose(
                        exp_t[j, b * 128 : (b + 1) * 128, a * 128 : (a + 1) * 128]
                    )
    with scope("s_stud_wait"):
        arrive(stud_copies[2])
        arrive(stud_copies[3])
        arrive(stud_near)
        student_block(at_x(1))
    with scope("s_xy1"):
        z_copies = rows_on_z(0, xy_copies)
    with scope("s_S_near"):
        student_block(at_x(3))
    with scope("s_S_far"):
        arrive(stud_far)
        student_block(at_x(2))
    with scope("s_P1"):
        arrive(proto_copy)
        left[0:k_dim, 0:cols] = proto_all[0]
        left[0:k_dim, cols:] = proto_all[1]
        left[k_dim:, :] = jnp.ones((16, both_cols), BF16)
        stud_sums = []
        for j in range(NX):
            value = jnp.dot(left[...], exp_s[j], preferred_element_type=F32)
            put_block(0, j, value[0:k_dim])
            stud_sums.append(value[k_dim : k_dim + 1])
        stud_xy = start_xy(xy_vec.at[1], jnp.concatenate(stud_sums, axis=1))
    with scope("s_col2"):
        sums = column_sums(0, z_copies)
    with scope("s_colx2"):
        scale = column_scale(1, sums)
    with scope("s_row2"):
        xy_copies = start_rows(1, scale)
        first1 = first_groups(0)
        for k in (2, 1, 3, 0):
            send_block(0, first1, k)
    with scope("s_studxy"):
        stud_z = start_z(z_vec.at[1], finish(xy_vec.at[1], stud_xy))
    with scope("s_xy2"):
        z_copies = rows_on_z(1, xy_copies)
    with scope("s_pass1"):
        pass_on_a(0, first1)
        pass_on_b(0, first1, 0)
        pass_on_b(0, first1, 1)

    with scope("s_col3"):
        sums = column_sums(1, z_copies)
    with scope("s_colx3"):
        col_copy = start_column_scale(2, sums)
        second1 = start_second(0, first1)
        scale = finish_column_scale(2, col_copy)
    with scope("s_P2"):
        for h in range(NC):
            left[0:k_dim, h * cols : (h + 1) * cols] = (
                proto_all[h].astype(F32) * scale[:, h * cols : (h + 1) * cols]
            ).astype(BF16)
        left[k_dim:, :] = split_rows(scale)
        first2 = first_groups(1)
        for k in (2, 1, 3, 0):
            j = at_x(k)
            value = jnp.dot(left[...], exp_t[j], preferred_element_type=F32)
            put_block(1, j, value[0:k_dim])
            send_block(1, first2, k)
            z_vec[0, z, :, pl.ds(pl.multiple_of(j * own, own), own)] = (
                value[k_dim : k_dim + 1] + value[k_dim + 1 : k_dim + 2]
            )
            cross[j] = jnp.sum(
                value[0:k_dim] * block_of(stud_all, j).astype(F32), axis=0, keepdims=True
            )
        z_copies = send_z(z_vec.at[0])
    with scope("s_pass2a"):
        pass_on_b(1, first2, 0)
        pass_on_a(1, first2)
    with scope("s_third1"):
        third1 = start_third(0, second1)
    with scope("s_pass2b"):
        pass_on_b(1, first2, 1)

    with scope("s_second2"):
        second2 = start_second(1, first2)
    with scope("s_z3"):
        xy_copies = start_xy(xy_vec.at[0], finish(z_vec.at[0], z_copies))

    with scope("s_dwS"):
        stud_total = finish(z_vec.at[1], stud_z)
        stud_factor = (1.0 / STUDENT_TEMP) / stud_total
        for h in range(NC):
            total = None
            for j in range(NX):
                weights = (
                    block_of(stud_all, j).astype(F32) * stud_factor[:, j * own : (j + 1) * own]
                ).astype(BF16)
                part = lax.dot_general(
                    weights,
                    exp_s[j, h * cols : (h + 1) * cols, :],
                    NT,
                    preferred_element_type=F32,
                )
                total = part if total is None else total + part
            dw_buf[h] = total
    with scope("s_third2"):
        third2 = start_third(1, second2)
    with scope("s_xy3"):
        row_scale = 1.0 / (total_rows * finish(xy_vec.at[0], xy_copies))
        teach_factor = (total_rows / STUDENT_TEMP) * row_scale

    with scope("s_loss"):
        part = None
        for j in range(NX):
            term = teach_factor[:, j * own : (j + 1) * own] * cross[j]
            for lane in range(0, own, 128):
                t = term[:, lane : lane + 128]
                part = t if part is None else part + t
        loss_xy = start_xy(xy_loss, part)

    with scope("s_mix"):
        part1 = finish_third(0, third1)
        part2 = finish_third(1, third2)
        for i in range(2 * NX):
            s = i * half_own
            fac_mix[0, i] = stud_factor[:, s : s + half_own]
            fac_mix[1, i] = teach_factor[:, s : s + half_own]
        mine = x * 2 + lax.rem(z, 2)
        ygather[y, z] = (fac_mix[0, mine] * part1 - fac_mix[1, mine] * part2).astype(BF16)
        NEAR, FAR = (1, 7, 2, 6), (3, 5, 4)
        gather_near = group(ygather.at[0, pl.ds(0, len(NEAR))])
        gather_far = group(ygather.at[0, pl.ds(0, len(FAR))])
        for g, steps in ((gather_far, FAR), (gather_near, NEAR)):
            for k in steps:
                send(g, ygather.at[y, z], ygather.at[y, z], z_dev(at_z(k)))
        gather_y = group(ygather.at[pl.ds(0, 3)])

        def forward(steps):
            for k in steps:
                sz = at_z(k)
                for h in AROUND:
                    send(gather_y, ygather.at[y, sz], ygather.at[y, sz], y_dev(at_y(h)))

    def teacher_half(h):
        total = None
        for j in range(NX):
            weights = (
                block_of(stud_all, j).astype(F32) * teach_factor[:, j * own : (j + 1) * own]
            ).astype(BF16)
            part = lax.dot_general(
                weights,
                exp_t[j, h * cols : (h + 1) * cols, :],
                NT,
                preferred_element_type=F32,
            )
            total = part if total is None else total + part
        dw_buf[h] = dw_buf[h] - total * scale[:, h * cols : (h + 1) * cols]

    with scope("s_dwT"):
        teacher_half(0)
    with scope("s_lossxy"):
        loss_z = start_z(z_loss, finish(xy_loss, loss_xy))
    with scope("s_dwT"):
        teacher_half(1)
        dw_send[...] = dw_buf[1 - c].astype(BF16)
        dw_copy = send_one(dw_send, dw_recv, partner)
    with scope("s_gatherz"):
        arrive(gather_near)
        forward((0, *NEAR))
        arrive(gather_far)
        forward(FAR)
    with scope("s_gp"):
        arrive(dw_copy)
        dw_hat = dw_buf[c] + dw_recv[...].astype(F32)
        proto_unit, proto_inverse = unit_along(proto_ref[...], 0)
        gp_ref[...] = (
            (total_cols / math.sqrt(total_rows))
            * proto_inverse
            * (dw_hat - proto_unit * jnp.sum(proto_unit * dw_hat, axis=0, keepdims=True))
        )
    with scope("s_lossz"):
        lse = jnp.log(stud_total)
        part = lse[:, 0:128]
        for lane in range(128, rows, 128):
            part = part + lse[:, lane : lane + 128]
        loss_x[c] = part - finish(z_loss, loss_z)
        loss_copy = send_one(loss_x.at[c], loss_x.at[c], partner)
    def sent(some):
        for g in some:
            copy_of(g, groups[g], groups[g], partner).wait_send()

    with scope("s_sent"):
        early = [g for g in range(len(groups)) if g not in (gather_y, loss_copy)]
        sent(early)
    with scope("s_gathery"):
        arrive(gather_y)
    with scope("s_dz"):
        for i in range(NY):
            for q in range(NZ):
                r = 16 * (q // 2)
                s = half_own * (q % 2)
                base = i * piece + r if r < piece else half_k + i * piece + r - piece
                dzt[base : base + 16, s : s + half_own] = ygather[i, q].astype(F32)
        dz = jnp.transpose(dzt[...])
        stud_unit, stud_inverse = unit_along(stud_ref[...], 1)
        gs_ref[...] = stud_inverse * (
            dz - stud_unit * jnp.sum(stud_unit * dz, axis=1, keepdims=True)
        )
    with scope("s_end"):
        arrive(loss_copy)
        loss_ref[...] = jnp.broadcast_to(
            jnp.sum(loss_x[0] + loss_x[1], axis=1, keepdims=True) / total_rows, loss_ref.shape
        )
        assert len(groups) == GROUPS, len(groups)
        sent((gather_y, loss_copy))


def store_kernel(*refs):
    results, outs, sem = refs[:3], refs[3:6], refs[6]
    for i, (result, out) in enumerate(zip(results, outs)):
        pltpu.make_async_copy(result, out, sem.at[i]).start()
    for i, (result, out) in enumerate(zip(results, outs)):
        pltpu.make_async_copy(result, out, sem.at[i]).wait()


def solution(mesh):
    def shards(teacher_emb, student_emb, prototypes):
        own, k_dim = teacher_emb.shape
        cols = prototypes.shape[1]
        rows, both = NX * own, 2 * cols
        total_rows = own * mesh.shape["dp"]
        total_cols = cols * mesh.shape["dp"] * mesh.shape["proto"]
        vmem = pltpu.VMEM
        piece = k_dim // 8
        scratch = [
            vmem((own, k_dim), BF16),
            vmem((k_dim, cols), BF16),
            vmem((NX, 4, own // 4, k_dim), BF16),
            vmem((NX, 4, k_dim, own // 4), BF16),
            vmem((NC, k_dim, cols), BF16),
            vmem((NC, cols, k_dim), BF16),
            vmem((k_dim + 16, both), BF16),
            vmem((NX, both, own), BF16),
            vmem((NX, own, both), BF16),
            vmem((NX, both, own), BF16),
            vmem((both, 128), F32),
            vmem((ITERS, NC, 1, both), F32),
            vmem((ITERS - 1, 2, NX * NY, 1, rows // 2), F32),
            vmem((ITERS - 1, 2, NZ, 1, rows // 2), F32),
            vmem((2, NX * NY, 1, rows), F32),
            vmem((2, NZ, 1, rows), F32),
            vmem((NX * NY, 1, 128), F32),
            vmem((NZ, 1, 128), F32),
            vmem((2, NX, 2, k_dim // 4, own), BF16),
            vmem((2, NY, 2, NX, piece // 2, own), BF16),
            vmem((2, 2, k_dim // 4, own), BF16),
            vmem((2, 2, NX, piece // 2, own), BF16),
            vmem((2, 2, k_dim // 4, own), BF16),
            vmem((2, 2, NX, piece // 2, own), BF16),
            vmem((2, 2, 2, k_dim // 4, own), BF16),
            vmem((2, 2, 2, NX, piece // 2, own), BF16),
            vmem((2, NY, piece, own), BF16),
            vmem((2, NX, piece, own), BF16),
            vmem((2, NY, piece, own), BF16),
            vmem((2, NX, piece, own), BF16),
            vmem((2, NZ, 16, own // 2), BF16),
            vmem((2, NZ, 16, own // 2), BF16),
            vmem((NY, NZ, 16, own // 2), BF16),
            vmem((NX, 1, own), F32),
            vmem((2, 2 * NX, 1, own // 2), F32),
            vmem((2, k_dim, cols), F32),
            vmem((k_dim, cols), BF16),
            vmem((k_dim, cols), BF16),
            vmem((2, 1, 128), F32),
            vmem((k_dim, own), F32),
            pltpu.SemaphoreType.DMA((GROUPS,)),
            pltpu.SemaphoreType.DMA((GROUPS,)),
            pltpu.SemaphoreType.DMA((3,)),
        ]
        anywhere = pl.BlockSpec(memory_space=pl.ANY)
        in_vmem = pl.BlockSpec(memory_space=vmem)
        shapes = ((1, 128), (own, k_dim), (k_dim, cols))
        results = pl.pallas_call(
            functools.partial(kernel, float(total_rows), float(total_cols)),
            out_shape=tuple(vmem(shape, F32) for shape in shapes),
            in_specs=[anywhere] * 3,
            out_specs=[in_vmem] * 3,
            scratch_shapes=scratch,
            compiler_params=pltpu.CompilerParams(
                collective_id=0, has_side_effects=True, vmem_limit_bytes=60 << 20
            ),
            name="prototype_head",
        )(teacher_emb.reshape(4, own // 4, k_dim), student_emb, prototypes)
        loss, grad_student, grad_prototypes = pl.pallas_call(
            store_kernel,
            out_shape=tuple(jax.ShapeDtypeStruct(shape, F32) for shape in shapes),
            in_specs=[in_vmem] * 3,
            out_specs=[anywhere] * 3,
            scratch_shapes=[pltpu.SemaphoreType.DMA((3,))],
            name="store_results",
        )(*(pltpu.with_memory_space_constraint(result, vmem) for result in results))
        return loss[0, 0], grad_student, grad_prototypes

    in_specs = (P("dp", None), P("dp", None), P(None, ("dp", "proto")))
    out_specs = (P(), P("dp", None), P(None, ("dp", "proto")))
    return jax.shard_map(shards, mesh=mesh, in_specs=in_specs, out_specs=out_specs, check_vma=False)
```
